512 devices in a mesh: gx: 8 (over y_lo, core), gy: 8 (over x, y_hi), gz: 8 (over z).
Axes of the slice: x: 4, y: 8 (y_hi: 2, y_lo: 4; y = y_hi * 4 + y_lo), z: 8, core: 2. Of those that a mesh axis runs over, the one named last changes fastest.
Arguments:
- particle_local_offsets: float32 [3, 16, 16, 32, 128], P(None, None, 'gx', 'gy', 'gz'), may hold values from 0 to 1, as said below
- particle_velocity: float32 [3, 16, 16, 32, 128], P(None, None, 'gx', 'gy', 'gz'), may hold values from -6 to 6
- stochastic_kicks: float32 [2, 3, 16, 16, 32, 128], P(None, None, None, 'gx', 'gy', 'gz'), may hold values from -6 to 6
- thermal_mesh_entry: int32 [16, 16, 32, 128], P(None, 'gx', 'gy', 'gz'), may hold values from 0 to 7, as said below
- occupant_tally: int32 [16, 32, 128], P('gx', 'gy', 'gz'), may hold values from 4 to 16
- fermion_thermal_level: float32 [32, 64, 256], P('gx', ('gy', 'gz')), may hold values from 0.35 to 6.3
- fluence_profile: float32 [32, 64], P('gx', ('gy', 'gz')), may hold values from 0.5 to 9
Outputs:
- new_positions: float32 [3, 16, 16, 32, 128], P(None, None, 'gx', 'gy', 'gz')
- new_velocities: float32 [3, 16, 16, 32, 128], P(None, None, 'gx', 'gy', 'gz')
- fermion_thermal_next: float32 [32, 64, 256], P('gx', ('gy', 'gz'))
The draws below stay inside these ranges and needn't reach their ends.
Inputs may be any that keep to these rules, and one draw needn't show every extreme that they name: `particle_local_offsets`: each component of a slot's offset lies in the half of the cell that thermal_mesh_entry names for it: [b/2, (b+1)/2) with b the bit of 4 bx + 2 by + bz for that component. `thermal_mesh_entry`: 4 bx + 2 by + bz for the half along x, y and depth of the cell in which the slot's atom starts.
All inputs are finite; a program needn't handle non-finite values.
Results may differ from the reference program's by a relative error of at most 0.0003.
Values sent between devices are 32-bit elements; how exact they have to be, the bound alone decides.
A program may use at most 192 MiB of HBM per device.

```python
import jax
import jax.numpy as jnp
from jax import lax

S = 16
STEPS = 2
SOLVER_SUBTIMES = 16
NCX = 16
NCY = 32
NCZ = 128
THERMAL_MESH_XAX = 32
THERMAL_MESH_YAX = 64
THERMAL_MESH_ZED = 256


def starting_halves(key):
    return jax.random.randint(key, (S, NCX, NCY, NCZ), 0, 8, dtype=jnp.int32)


def cold_rows(key):
    key = jax.random.fold_in(key, 5)
    phase = jax.random.randint(key, (), 0, 16, dtype=jnp.int32)
    rows = jnp.arange(THERMAL_MESH_YAX, dtype=jnp.int32)
    return (rows - phase) % 16 < 3


def draw_thermal_mesh_entry(key, part):
    return starting_halves(key)


def draw_particle_local_offsets(key, part):
    halves = starting_halves(key)
    key = jax.random.fold_in(key, 7)
    inside = jax.random.uniform(key, (3, S, NCX, NCY, NCZ), jnp.float32)
    half_bits = jnp.stack([halves // 4, halves // 2 % 2, halves % 2]).astype(jnp.float32)
    return 0.5 * (half_bits + inside)


def draw_fermion_thermal_level(key, part):
    banded = cold_rows(key)[None, :, None]
    key = jax.random.fold_in(key, 11)
    shape = (THERMAL_MESH_XAX, THERMAL_MESH_YAX, THERMAL_MESH_ZED)
    factor = jax.random.uniform(key, shape, jnp.float32, 0.7, 1.4)
    return jnp.where(banded, 0.5, 4.0).astype(jnp.float32) * factor


def draw_fluence_profile(key, part):
    banded = cold_rows(key)[None, :]
    key = jax.random.fold_in(key, 13)
    shape = (THERMAL_MESH_XAX, THERMAL_MESH_YAX)
    factor = jnp.exp(jax.random.uniform(key, shape, jnp.float32, 0.0, 0.69314718))
    return jnp.where(banded, 0.5, 4.5).astype(jnp.float32) * factor


def with_ends(values, rng, low, high):
    longest = values.shape.index(max(values.shape))
    spots = []
    for shift in (0, 1):
        where = [jax.random.randint(jax.random.fold_in(rng, axis), (), 0, length) for axis, length in enumerate(values.shape)]
        where[longest] = (where[longest] + shift) % values.shape[longest]
        spots.append(tuple(where))
    return values.at[spots[0]].set(low).at[spots[1]].set(high)


def shard_levels(stream_key, shape, cuts, smallest, top_value):
    factor_of = 1.0
    for dim, blocks in cuts:
        heights = jax.random.uniform(jax.random.fold_in(jax.random.fold_in(stream_key, 6), dim), (blocks,), jnp.float32, smallest / len(cuts), top_value / len(cuts))
        factor_of = factor_of * jnp.repeat(jnp.exp(heights), shape[dim] // blocks).reshape((-1,) + (1,) * (len(shape) - 1 - dim))
    return factor_of


def bell_draw(key, shape, deviation, bound, shards=(), kind=jnp.bfloat16):
    drawn = jax.random.normal(key, shape, jnp.float32) * deviation
    if len(shards) > 0:
        drawn = shard_levels(key, shape, shards, -0.22, 0.18) * drawn
    return jnp.clip(drawn, min=-bound, max=bound).astype(kind)


def setup_inputs(seed: int = 0) -> dict:
    seeds = jax.random.split(jax.random.key(seed), 8)
    return {
        "particle_local_offsets": draw_particle_local_offsets(jax.random.fold_in(seeds[7], 71), 0),
        "particle_velocity": bell_draw(seeds[1], (3, S, NCX, NCY, NCZ), 1.0, 6.0, ((2, 8), (3, 8), (4, 8)), jnp.float32),
        "stochastic_kicks": bell_draw(seeds[2], (STEPS, 3, S, NCX, NCY, NCZ), 1.0, 6.0, ((3, 8), (4, 8), (5, 8)), jnp.float32),
        "thermal_mesh_entry": draw_thermal_mesh_entry(jax.random.fold_in(seeds[7], 71), 0),
        "occupant_tally": with_ends(jax.random.randint(seeds[4], (NCX, NCY, NCZ), S // 4, S + 1), jax.random.fold_in(seeds[4], 1), S // 4, S).astype(jnp.int32),
        "fermion_thermal_level": draw_fermion_thermal_level(jax.random.fold_in(seeds[7], 71), 0),
        "fluence_profile": draw_fluence_profile(jax.random.fold_in(seeds[7], 71), 0),
    }


CLOCK_INCREMENT = 0.03
DRAG_RATE = 1.0
DENSITY_DECAY = 2.0
PAIR_SCALE = 1.0
PAIR_DECAY = 3.0
EMBEDDING = 10.0
SPECIFIC_WARMING = 2.0
DIFFUSION = 0.08
LASER_GAIN = 0.02
NEIGHBOUR_CELLS = [(along_x, along_y, along_z) for along_x in (-1, 0, 1) for along_y in (-1, 0, 1) for along_z in (-1, 0, 1)]

def pair_weights(squared):
    reach_left = jnp.maximum(1.0 - squared, 0.0)
    spread = jnp.exp(-DENSITY_DECAY * squared)
    repulse = PAIR_SCALE * jnp.exp(-PAIR_DECAY * squared)
    density = spread * reach_left * reach_left
    density_slope = spread * (-DENSITY_DECAY * reach_left * reach_left - 2.0 * reach_left)
    pair_slope = repulse * (-PAIR_DECAY * reach_left * reach_left - 2.0 * reach_left)
    return (density, density_slope, pair_slope)

def embedding_slope(density):
    return -0.5 * EMBEDDING / jnp.sqrt(1.0 + density)

def conductivity(current):
    squared = current * current
    return 1.0 + squared / (1.0 + squared)

def shifted(field, delta_cell):
    rank = field.ndim
    moved = jnp.roll(field, (-delta_cell[0], -delta_cell[1]), axis=(rank - 3, rank - 2))
    widths = [(0, 0)] * (rank - 1) + [(1, 1)]
    padded = jnp.pad(moved, widths)
    return lax.slice_in_dim(padded, 1 + delta_cell[2], 1 + delta_cell[2] + field.shape[-1], axis=rank - 1)

def coupled_partitions(grid_cells):
    cells_x = grid_cells.shape[0] // 2
    cells_y = grid_cells.shape[1] // 2
    cells_z = grid_cells.shape[2] // 2
    return grid_cells.reshape(cells_x, 2, cells_y, 2, cells_z, 2).transpose(1, 3, 5, 0, 2, 4).reshape(8, cells_x, cells_y, cells_z)

def grid_of(halves):
    cells_x, cells_y, cells_z = (halves.shape[1], halves.shape[2], halves.shape[3])
    return halves.reshape(2, 2, 2, cells_x, cells_y, cells_z).transpose(3, 0, 4, 1, 5, 2).reshape(2 * cells_x, 2 * cells_y, 2 * cells_z)

def densities(atom_data):
    slot_order = jnp.arange(atom_data.shape[1], dtype=jnp.int32)
    summed = jnp.zeros(atom_data.shape[1:], jnp.float32)
    for delta_cell in NEIGHBOUR_CELLS:
        neighbour = shifted(atom_data, delta_cell)
        offset = jnp.array(delta_cell, jnp.float32).reshape(3, 1, 1, 1, 1)

        def one_slot(slot_index, neighbour=neighbour, offset=offset, delta_cell=delta_cell):
            home_atom = lax.dynamic_index_in_dim(atom_data[:3], slot_index, axis=1, keepdims=True)
            separation = neighbour[:3] + offset - home_atom
            squared = lax.optimization_barrier(jnp.sum(separation * separation, axis=0))
            density = pair_weights(squared)[0]
            present = neighbour[3]
            if delta_cell == (0, 0, 0):
                present = present * (slot_order != slot_index).astype(jnp.float32)[:, None, None, None]
            return lax.optimization_barrier(jnp.sum(density * present, axis=0))
        summed = summed + lax.map(one_slot, slot_order)
    return summed * atom_data[3]

def forces_of(atom_data, slopes):
    slot_order = jnp.arange(atom_data.shape[1], dtype=jnp.int32)
    summed = jnp.zeros((atom_data.shape[1], 3) + atom_data.shape[2:], jnp.float32)
    for delta_cell in NEIGHBOUR_CELLS:
        neighbour = shifted(atom_data, delta_cell)
        far_slope = shifted(slopes, delta_cell)
        offset = jnp.array(delta_cell, jnp.float32).reshape(3, 1, 1, 1, 1)

        def one_slot(slot_index, neighbour=neighbour, far_slope=far_slope, offset=offset, delta_cell=delta_cell):
            home_atom = lax.dynamic_index_in_dim(atom_data[:3], slot_index, axis=1, keepdims=True)
            own_slope = lax.dynamic_index_in_dim(slopes, slot_index, axis=0, keepdims=True)
            separation = neighbour[:3] + offset - home_atom
            squared = lax.optimization_barrier(jnp.sum(separation * separation, axis=0))
            weights = pair_weights(squared)
            present = neighbour[3]
            if delta_cell == (0, 0, 0):
                present = present * (slot_order != slot_index).astype(jnp.float32)[:, None, None, None]
            strength = ((own_slope + far_slope) * weights[1] + weights[2]) * present
            return 2.0 * lax.optimization_barrier(jnp.sum(strength[None] * separation, axis=1))
        summed = summed + lax.map(one_slot, slot_order)
    return jnp.transpose(summed, (1, 0, 2, 3, 4)) * atom_data[3][None]

def reference(particle_local_offsets, particle_velocity, stochastic_kicks, thermal_mesh_entry, occupant_tally, fermion_thermal_level, fluence_profile):
    slot_order = jnp.arange(particle_local_offsets.shape[1], dtype=jnp.int32)
    occupied = (slot_order[:, None, None, None] < occupant_tally[None]).astype(jnp.float32)
    interior_partition = thermal_mesh_entry[None] == jnp.arange(8, dtype=jnp.int32)[:, None, None, None, None]
    nuclei_thermal_level = lax.optimization_barrier(jnp.sum(jnp.where(interior_partition, coupled_partitions(fermion_thermal_level)[:, None], 0.0), axis=0))
    handed_over = jnp.zeros(occupied.shape, jnp.float32)
    for momentum_total in range(STEPS):
        atom_data = jnp.concatenate([particle_local_offsets, occupied[None]], axis=0)
        slopes = embedding_slope(densities(atom_data))
        forces = forces_of(atom_data, slopes)
        jolted_speeds = particle_velocity + CLOCK_INCREMENT * forces
        slowed_speeds = (1.0 - DRAG_RATE * CLOCK_INCREMENT) * jolted_speeds + jnp.sqrt(2.0 * DRAG_RATE * CLOCK_INCREMENT * nuclei_thermal_level)[None] * stochastic_kicks[momentum_total]
        handed_over = handed_over + occupied * 0.5 * (lax.optimization_barrier(jnp.sum(jolted_speeds * jolted_speeds, axis=0)) - lax.optimization_barrier(jnp.sum(slowed_speeds * slowed_speeds, axis=0)))
        particle_velocity = occupied[None] * slowed_speeds + (1.0 - occupied[None]) * particle_velocity
        particle_local_offsets = particle_local_offsets + CLOCK_INCREMENT * (occupied[None] * slowed_speeds)
    optical_power_source = grid_of(lax.optimization_barrier(jnp.sum(jnp.where(interior_partition, handed_over[None], 0.0), axis=1)))
    excited_fermions = fermion_thermal_level + optical_power_source / SPECIFIC_WARMING
    vertical_mesh_index = fermion_thermal_level.shape[2]
    depth_decay = jnp.exp(-(jnp.arange(vertical_mesh_index).astype(jnp.float32) + 0.5) / (0.25 * vertical_mesh_index))
    source = LASER_GAIN * fluence_profile[:, :, None] * depth_decay[None, None, :]

    def conduction_sweep(substep_index, current):
        conduct = conductivity(current)
        net_flow = []
        for along_axis in (0, 1):
            upper_flux = 0.5 * (conduct + jnp.roll(conduct, -1, along_axis)) * (jnp.roll(current, -1, along_axis) - current)
            net_flow.append(upper_flux - jnp.roll(upper_flux, 1, along_axis))
        face_flux = 0.5 * (conduct[:, :, :-1] + conduct[:, :, 1:]) * (current[:, :, 1:] - current[:, :, :-1])
        zero_face = jnp.zeros(face_flux.shape[:2] + (1,), jnp.float32)
        depth_flow = jnp.concatenate([face_flux, zero_face], axis=2) - jnp.concatenate([zero_face, face_flux], axis=2)
        return current + DIFFUSION * (net_flow[0] + net_flow[1] + depth_flow) + source
    return (particle_local_offsets, particle_velocity, lax.fori_loop(0, SOLVER_SUBTIMES, conduction_sweep, excited_fermions))
```

```python
import itertools

import jax
import jax.numpy as jnp
from jax import lax
from jax.experimental import pallas as pl
from jax.experimental.pallas import tpu as pltpu
from jax.sharding import PartitionSpec as P

MESH = pl.DeviceIdType.MESH
F32 = jnp.float32
STEPS = 2
HALO = 8
ROUNDS = 16 // HALO
REACH = HALO // 4
FAR = 1.0e6
CUBE = [d for d in itertools.product((-1, 0, 1), repeat=3)]
AROUND = [d for d in CUBE if d != (0, 0, 0)]
WIDE = [
    d
    for d in itertools.product(range(-REACH, REACH + 1), (-1, 0, 1), (-1, 0, 1))
    if d != (0, 0, 0)
]
FULL = 8 * 3


def parts_of(pieces):
    rows, start = {}, 0
    for d in AROUND:
        if d[2] != 0:
            count = 8
        elif d[1] != 0:
            count = 8 * ((pieces + 3) // 4)
        else:
            count = 8 * pieces
        rows[d] = (start, count)
        start += count
    return rows, start


POS_ROWS, POS_TOTAL = parts_of(6)
SLOPE_ROWS, SLOPE_TOTAL = parts_of(2)


def turn(block, shift, axis=1):
    size = block.shape[axis]
    shift = shift % size
    return block if shift == 0 else pltpu.roll(block, shift, axis)


def lanes(rows=8):
    return lax.broadcasted_iota(jnp.int32, (rows, 128), 1)


def pieces_of(block):
    return [block[8 * k : 8 * k + 8] for k in range(block.shape[0] // 8)]


def packed(pieces):
    lane = lanes()
    y, z = (lane >> 4) & 3, lane & 15
    faces = {}
    for dz in (1, -1):
        face = pieces[0]
        for k, piece in enumerate(pieces):
            moved = turn(piece, k - 15 if dz == 1 else k)
            face = moved if k == 0 else jnp.where(z == k, moved, face)
        faces["z", dz] = [face]
    for dy in (1, -1):
        blocks = []
        for first in range(0, len(pieces), 4):
            face = None
            for k, piece in enumerate(pieces[first : first + 4]):
                moved = turn(piece, 16 * k - 48 if dy == 1 else 16 * k)
                face = moved if face is None else jnp.where(y == k, moved, face)
            blocks.append(face)
        faces["y", dy] = blocks
    return faces


def face_start(table, d):
    return table[d][0], table[d][1]


def neighbours(own, landed, table, blank_low, blank_high, put):
    lane = lanes()
    x, y, z = lane >> 6, (lane >> 4) & 3, lane & 15
    count = len(own)

    def column(dx, dy, dz):
        if (dx, dy, dz) == (0, 0, 0):
            return own
        start, rows = table[dx, dy, dz]
        return pieces_of(landed[start : start + rows])

    for ex in (-1, 0, 1):

        def along_x(dy, dz):
            here = column(0, dy, dz)
            if ex == 0:
                return here
            there = column(ex, dy, dz)
            if ex == 1:
                return [turn(jnp.where(x == 0, b, a), 64) for a, b in zip(here, there)]
            return [turn(jnp.where(x == 0, a, b), 64) for a, b in zip(here, there)]

        flat = {dy: along_x(dy, 0) for dy in (-1, 0, 1)}
        deep = {(dy, dz): along_x(dy, dz)[0] for dy in (-1, 0, 1) for dz in (-1, 1)}
        for dy in (-1, 0, 1):
            if blank_low is not None:
                deep[dy, -1] = jnp.where(blank_low, FAR, deep[dy, -1])
                deep[dy, 1] = jnp.where(blank_high, FAR, deep[dy, 1])
        for ey in (-1, 0, 1):
            if ey == 0:
                level = flat[0]
                ends = {dz: deep[0, dz] for dz in (-1, 1)}
            elif ey == 1:
                level = [
                    jnp.where(y == 3, turn(flat[1][k // 4], 48 - 16 * (k % 4)), turn(flat[0][k], -16))
                    for k in range(count)
                ]
                ends = {
                    dz: jnp.where(y == 3, turn(deep[1, dz], 48), turn(deep[0, dz], -16))
                    for dz in (-1, 1)
                }
            else:
                level = [
                    jnp.where(y == 0, turn(flat[-1][k // 4], -16 * (k % 4)), turn(flat[0][k], 16))
                    for k in range(count)
                ]
                ends = {
                    dz: jnp.where(y == 0, turn(deep[-1, dz], -48), turn(deep[0, dz], 16))
                    for dz in (-1, 1)
                }
            put((ex, ey, 0), level)
            put(
                (ex, ey, 1),
                [jnp.where(z == 15, turn(ends[1], 15 - k), turn(level[k], -1)) for k in range(count)],
            )
            put(
                (ex, ey, -1),
                [jnp.where(z == 0, turn(ends[-1], -k), turn(level[k], 1)) for k in range(count)],
            )


def kernel(
    first_ref, rest_ref, heat_ref,
    moved_ref, grid_ref,
    first, rest, heat, position, velocity, shown, near, near_slope, density, force,
    pos_face, pos_land, slope_face, slope_land, level_ref, handed,
    tile_out, tile_land_a, tile_land_b, tile_out_b, ext_a, ext_b, ext_src,
    back_out, back_land, row_out, row_land,
    first_sem, heat_sem, pos_sem, slope_sem, tile_sem, back_sem, row_sem,
):
    gx, gy, gz = (lax.axis_index(a) for a in ("gx", "gy", "gz"))

    def x_place(tx):
        ring = lax.rem(tx + 1, 8)
        return lax.rem(ring, 2), (ring // 2) * 2

    def y_place(ty):
        return lax.rem(ty, 4) * 2, ty // 4

    def device(xp, yp, tz):
        return (xp[0] + yp[0], xp[1] + yp[1], tz)

    ring_place = (gy // 2) * 2 + lax.rem(gx, 2)
    tx = lax.rem(ring_place + 7, 8)
    ty = lax.rem(gy, 2) * 4 + gx // 2
    tz = gz
    xs = {d: x_place(lax.rem(tx + d + 8, 8)) for d in range(-2, 3)}
    ys = {d: y_place(lax.rem(ty + d + 8, 8)) for d in (-1, 0, 1)}
    zs = {d: lax.rem(tz + d + 8, 8) for d in (-1, 0, 1)}

    def partner(d):
        return device(xs[d[0]], ys[d[1]], zs[d[2]])

    my_x, my_y = x_place(gx), y_place(gy)

    def worker(z):
        return device(my_x, my_y, z)

    def owner(z):
        return (tx, ty, z)

    barrier = pltpu.get_barrier_semaphore()
    greeted = [worker(z) for z in range(8)] + [owner(z) for z in range(8)]
    greeted += [partner(d) for d in (WIDE if REACH > 1 else AROUND)]
    for target in greeted:
        pl.semaphore_signal(barrier, inc=1, device_id=target, device_id_type=MESH)
    pl.semaphore_wait(barrier, len(greeted))

    def send(src, dst, sems, target):
        pltpu.make_async_remote_copy(
            src_ref=src, dst_ref=dst, send_sem=sems.at[0], recv_sem=sems.at[1],
            device_id=target, device_id_type=MESH,
        ).start()

    def take(ref, sem):
        pltpu.make_async_copy(ref, ref, sem).wait()

    send(first_ref, first, first_sem.at[0], worker(gz))
    for z in range(8):
        send(heat_ref.at[z], heat.at[gz], heat_sem, worker(z))
    send(rest_ref, rest, first_sem.at[1], worker(gz))

    lane = lanes()
    row = lax.broadcasted_iota(jnp.int32, (8, 128), 0)
    slot = lax.broadcasted_iota(jnp.int32, (16, 128), 0)

    take(first, first_sem.at[0, 1])
    live = slot.astype(F32) < first[48:49, :]
    live3 = jnp.concatenate([live] * 3, axis=0)
    position[...] = first[0:48, :]
    at_bottom, at_top = tz == 0, tz == 7

    def spread(own, faces, face_ref, land, table, sems):
        at = 0
        places = {}
        for key, blocks in [(("x", 0), own)] + list(faces.items()):
            for k, block in enumerate(blocks):
                face_ref[at + 8 * k : at + 8 * k + 8, :] = block
            places[key] = (at, 8 * len(blocks))
            at += 8 * len(blocks)
        for d in AROUND:
            key = ("z", d[2]) if d[2] else ("y", d[1]) if d[1] else ("x", 0)
            start, rows = places[key]
            there = tuple(-c for c in d)
            send(
                face_ref.at[pl.ds(start, rows)], land.at[pl.ds(table[there][0], rows)],
                sems, partner(d),
            )

    handed[...] = jnp.zeros((16, 128), F32)

    def dynamics(step, carry):
        own = pieces_of(jnp.where(live3, position[...], FAR))
        for k, piece in enumerate(own):
            shown[8 * k : 8 * k + 8, :] = piece
        spread(own, packed(own), pos_face.at[step], pos_land.at[step], POS_ROWS, pos_sem.at[step])
        take(pos_land.at[step], pos_sem.at[step, 1])

        def put_position(e, pieces):
            index = CUBE.index(e)
            for k, piece in enumerate(pieces):
                near[index, 8 * k : 8 * k + 8, :] = piece + float(e[k // 2])

        landed = pos_land[step]
        neighbours(own, landed, POS_ROWS, at_bottom, at_top, put_position)

        def one_density(s, carry):
            home = [shown[pl.ds(16 * c + s, 1), :] for c in range(3)]
            total = jnp.zeros((16, 128), F32)
            for index in range(27):
                d = [near[index, 16 * c : 16 * c + 16, :] - home[c] for c in range(3)]
                q = d[0] * d[0] + d[1] * d[1] + d[2] * d[2]
                w = jnp.maximum(1.0 - q, 0.0)
                total = total + jnp.exp(-2.0 * q) * (w * w)
            density[pl.ds(s, 1), :] = jnp.sum(total, axis=0, keepdims=True)
            return carry

        lax.fori_loop(0, 16, one_density, 0)
        rho = jnp.where(live, density[...] - 1.0, 0.0)
        slope = -10.0 * lax.rsqrt(1.0 + jnp.maximum(rho, 0.0))
        density[...] = slope
        own_slope = pieces_of(slope)
        spread(
            own_slope, packed(own_slope), slope_face.at[step], slope_land.at[step], SLOPE_ROWS,
            slope_sem.at[step],
        )
        take(slope_land.at[step], slope_sem.at[step, 1])

        def put_slope(e, pieces):
            index = CUBE.index(e)
            for k, piece in enumerate(pieces):
                near_slope[index, 8 * k : 8 * k + 8, :] = piece

        neighbours(own_slope, slope_land[step], SLOPE_ROWS, None, None, put_slope)

        def one_force(s, carry):
            home = [shown[pl.ds(16 * c + s, 1), :] for c in range(3)]
            home_slope = density[pl.ds(s, 1), :]
            total = [jnp.zeros((16, 128), F32) for _ in range(3)]
            for index in range(27):
                d = [near[index, 16 * c : 16 * c + 16, :] - home[c] for c in range(3)]
                q = d[0] * d[0] + d[1] * d[1] + d[2] * d[2]
                w = jnp.maximum(1.0 - q, 0.0)
                once = jnp.exp(-q)
                both = near_slope[index] + home_slope
                strength = (w * (once * once)) * (both * (w + 1.0) + once * (3.0 * w + 2.0))
                total = [t + strength * c for t, c in zip(total, d)]
            for c in range(3):
                force[pl.ds(16 * c + s, 1), :] = jnp.sum(total[c], axis=0, keepdims=True)
            return carry

        lax.fori_loop(0, 16, one_force, 0)

        @pl.when(step == 0)
        def _():
            take(rest, first_sem.at[1, 1])
            take(heat, heat_sem.at[1])
            velocity[...] = rest[0:48, :]
            entry = rest[144:160, :]
            tile = heat[:, 0, :]
            level = jnp.zeros((16, 128), F32)
            for bx, bz in itertools.product((0, 1), repeat=2):
                spread_out = jnp.dot(
                    tile, choice(bx, bz), precision=lax.Precision.HIGHEST, preferred_element_type=F32
                )
                for by in (0, 1):
                    mine = row == 2 * ((lane >> 4) & 3) + by
                    half = jnp.sum(jnp.where(mine, spread_out, 0.0), axis=0, keepdims=True)
                    level = level + jnp.where(entry == float(4 * bx + 2 * by + bz), half, 0.0)
            level_ref[...] = jnp.sqrt(0.06 * level)

        old = velocity[...]
        kicks = rest[pl.ds(pl.multiple_of(48 + 48 * step, 16), 48), :]
        kicked = old + 0.03 * jnp.where(live3, -2.0 * force[...], 0.0)
        noise = jnp.concatenate([level_ref[...]] * 3, axis=0)
        damped = 0.97 * kicked + noise * kicks
        gain = kicked * kicked - damped * damped
        handed[...] += jnp.where(live, 0.5 * (gain[0:16] + gain[16:32] + gain[32:48]), 0.0)
        velocity[...] = jnp.where(live3, damped, old)
        position[...] += 0.03 * jnp.where(live3, damped, 0.0)
        return carry

    def choice(bx, bz):
        source = lax.broadcasted_iota(jnp.int32, (128, 128), 0)
        target = lax.broadcasted_iota(jnp.int32, (128, 128), 1)
        wanted = (2 * (target >> 6) + bx) * 32 + 2 * (target & 15) + bz
        return jnp.where(source == wanted, 1.0, 0.0).astype(F32)

    lax.fori_loop(0, STEPS, dynamics, 0)

    back_out[0:48, :] = position[...]
    back_out[48:96, :] = velocity[...]
    send(back_out, back_land, back_sem, owner(tz))

    deposit = jnp.zeros((8, 128), F32)
    entry = rest[144:160, :]
    for bx, bz in itertools.product((0, 1), repeat=2):
        low, high = (
            jnp.sum(
                jnp.where(entry == float(4 * bx + 2 * by + bz), handed[...], 0.0), axis=0, keepdims=True
            )
            for by in (0, 1)
        )
        rows_y = jnp.where((row & 1) == 1, high, low)
        placed = jnp.where((row >> 1) == ((lane >> 4) & 3), rows_y, 0.0)
        deposit = deposit + lax.dot_general(
            placed, choice(bx, bz), (((1,), (1,)), ((), ())),
            precision=lax.Precision.HIGHEST, preferred_element_type=F32,
        )
    tile_out[0:8, :] = heat[:, 0, :] + 0.5 * deposit
    tile_out[8:16, :] = heat[:, 1, :]

    width = 4 + 2 * HALO
    part = lane >> 5
    depth = lax.broadcasted_iota(jnp.int32, (24, 128), 1) + (32 * tz - 32)
    inner_face = (depth >= 0) & (depth < 255)

    def extend(tile_of, ext):
        for xx in range(width):
            xt, xi = (xx - HALO) // 4, (xx - HALO) % 4
            for yt in (-1, 0, 1):
                low, mid, high = (
                    turn(tile_of((xt, yt, zt)), 32 * (zt + 1) - 32 * xi) for zt in (-1, 0, 1)
                )
                ext[xx, 8 * yt + 8 : 8 * yt + 16, :] = jnp.where(
                    part == 0, low, jnp.where(part == 1, mid, high)
                )

    def sweep(src, dst):
        def conduct(t):
            return 2.0 - 1.0 / (1.0 + t * t)

        here = src[0]
        k_here = conduct(here)
        before = None
        for xx in range(width):
            after = None
            if xx < width - 1:
                ahead = src[xx + 1]
                k_ahead = conduct(ahead)
                after = (k_here + k_ahead) * (ahead - here)
            if 0 < xx < width - 1:
                up_y = (k_here + turn(k_here, -1, 0)) * (turn(here, -1, 0) - here)
                up_z = (k_here + turn(k_here, -1)) * (turn(here, -1) - here)
                up_z = jnp.where(inner_face, up_z, 0.0)
                net = (after - before) + (up_y - turn(up_y, 1, 0)) + (up_z - turn(up_z, 1))
                dst[xx] = here + 0.04 * net + ext_src[xx]
            before = after
            if xx < width - 1:
                here, k_here = ahead, k_ahead

    def centre(ext):
        tile = None
        for xi in range(4):
            moved = turn(ext[HALO + xi, 8:16, :], 32 * xi - 32)
            tile = moved if tile is None else jnp.where(part == xi, moved, tile)
        return tile

    for turn_of in range(ROUNDS):
        out = tile_out if turn_of == 0 else tile_out_b.at[turn_of - 1]
        land = tile_land_a if turn_of == 0 else tile_land_b.at[turn_of - 1]
        if turn_of:
            out[...] = centre(ext_a)
        for index, d in enumerate(WIDE):
            there = WIDE.index(tuple(-c for c in d))
            send(out, land.at[there], tile_sem.at[turn_of], partner(d))
        take(land, tile_sem.at[turn_of, 1])
        extend(lambda d: out[0:8, :] if d == (0, 0, 0) else land[WIDE.index(d), 0:8, :], ext_a)
        if turn_of == 0:
            extend(
                lambda d: out[8:16, :] if d == (0, 0, 0) else land[WIDE.index(d), 8:16, :], ext_src
            )
            for edge in (0, width - 1):
                ext_b[edge] = ext_a[edge]

        def two(i, carry):
            sweep(ext_a, ext_b)
            sweep(ext_b, ext_a)
            return carry

        lax.fori_loop(0, HALO // 2, two, 0)

    result = centre(ext_a)
    for y in range(8):
        row_out[y, :, :] = result[y : y + 1]
        send(row_out.at[y], row_land.at[tz], row_sem, owner(y))

    take(back_land, back_sem.at[1])
    moved_ref[...] = back_land[...]
    take(row_land, row_sem.at[1])
    grid_ref[...] = row_land[...]

    take(first_ref, first_sem.at[0, 0])
    take(rest_ref, first_sem.at[1, 0])
    take(heat_ref, heat_sem.at[0])
    for step in range(STEPS):
        take(pos_land.at[step], pos_sem.at[step, 0])
        take(slope_land.at[step], slope_sem.at[step, 0])
    take(tile_land_a, tile_sem.at[0, 0])
    for turn_of in range(1, ROUNDS):
        take(tile_land_b.at[turn_of - 1], tile_sem.at[turn_of, 0])
    take(back_out, back_sem.at[0])
    take(row_out, row_sem.at[0])


def face_rows(pieces):
    return 8 * (pieces + 2 + 2 * ((pieces + 3) // 4))


def shards(
    particle_local_offsets,
    particle_velocity,
    stochastic_kicks,
    thermal_mesh_entry,
    occupant_tally,
    fermion_thermal_level,
    fluence_profile,
):
    first = jnp.concatenate(
        [
            particle_local_offsets.reshape(48, 128),
            jnp.broadcast_to(occupant_tally.astype(F32).reshape(1, 128), (8, 128)),
        ]
    )
    rest = jnp.concatenate(
        [
            particle_velocity.reshape(48, 128),
            stochastic_kicks.reshape(96, 128),
            thermal_mesh_entry.astype(F32).reshape(16, 128),
        ]
    )
    depth = fermion_thermal_level.shape[2]
    decay = jnp.exp(-(jnp.arange(depth).astype(F32) + 0.5) / (0.25 * depth))
    source = 0.02 * fluence_profile[:, :, None] * decay[None, None, :]
    heat = jnp.stack([fermion_thermal_level[:, 0], source[:, 0]], axis=0)
    heat = heat.reshape(2, 4, 8, 32).transpose(2, 0, 1, 3).reshape(8, 2, 128)

    width = 4 + 2 * HALO
    vmem = pl.BlockSpec(memory_space=pltpu.VMEM)
    buffers = [
        (56, 128), (160, 128), (8, 2, 128), (48, 128), (48, 128), (48, 128),
        (27, 48, 128), (27, 16, 128), (16, 128), (48, 128),
        (STEPS, face_rows(6), 128), (STEPS, POS_TOTAL, 128),
        (STEPS, face_rows(2), 128), (STEPS, SLOPE_TOTAL, 128),
        (16, 128), (16, 128),
        (16, 128), (len(WIDE), 16, 128), (ROUNDS - 1, len(WIDE), 8, 128), (ROUNDS - 1, 8, 128),
        (width, 24, 128), (width, 24, 128), (width, 24, 128),
        (96, 128), (96, 128), (8, 1, 128), (8, 1, 128),
    ]
    sems = [(2, 2), (2,), (STEPS, 2), (STEPS, 2), (ROUNDS, 2), (2,), (2,)]
    moved, grid = pl.pallas_call(
        kernel,
        out_shape=(
            jax.ShapeDtypeStruct((96, 128), F32),
            jax.ShapeDtypeStruct((8, 1, 128), F32),
        ),
        in_specs=[vmem] * 3,
        out_specs=(vmem, vmem),
        scratch_shapes=[pltpu.VMEM(shape, F32) for shape in buffers]
        + [pltpu.SemaphoreType.DMA(shape) for shape in sems],
        compiler_params=pltpu.CompilerParams(
            collective_id=0, has_side_effects=True, vmem_limit_bytes=32 * 1024 * 1024
        ),
    )(first, rest, heat)
    shape = particle_local_offsets.shape
    grid = grid.reshape(8, 4, 32).transpose(1, 0, 2).reshape(4, 1, 256)
    return moved[:48].reshape(shape), moved[48:].reshape(shape), grid


def solution(mesh):
    placed = (
        P(None, None, "gx", "gy", "gz"),
        P(None, None, "gx", "gy", "gz"),
        P(None, None, None, "gx", "gy", "gz"),
        P(None, "gx", "gy", "gz"),
        P("gx", "gy", "gz"),
        P("gx", ("gy", "gz"), None),
        P("gx", ("gy", "gz")),
    )
    return jax.shard_map(
        shards,
        mesh=mesh,
        in_specs=placed,
        out_specs=(
            P(None, None, "gx", "gy", "gz"),
            P(None, None, "gx", "gy", "gz"),
            P("gx", ("gy", "gz"), None),
        ),
        check_vma=False,
    )
```

```python
import itertools

import jax
import jax.numpy as jnp
from jax import lax
from jax.experimental import pallas as pl
from jax.experimental.pallas import tpu as pltpu
from jax.sharding import PartitionSpec as P

MESH = pl.DeviceIdType.MESH
F32 = jnp.float32
STEPS = 2
HALO = 8
ROUNDS = 16 // HALO
REACH = HALO // 4
FAR = 1.0e6
CUBE = [d for d in itertools.product((-1, 0, 1), repeat=3)]
AROUND = sorted((d for d in CUBE if d != (0, 0, 0)), key=lambda d: -sum(map(abs, d)))
WIDE = sorted(
    (
        d
        for d in itertools.product(range(-REACH, REACH + 1), (-1, 0, 1), (-1, 0, 1))
        if d != (0, 0, 0)
    ),
    key=lambda d: -sum(map(abs, d)),
)
FOLD = (4 + 2 * HALO) // 2
FLAT = [d for d in WIDE if d[2] == 0]


def parts_of(pieces):
    rows, start = {}, 0
    for d in AROUND:
        if d[2] != 0:
            count = 8
        elif d[1] != 0:
            count = 8 * ((pieces + 3) // 4)
        else:
            count = 8 * pieces
        rows[d] = (start, count)
        start += count
    return rows, start


POS_ROWS, POS_TOTAL = parts_of(6)
SLOPE_ROWS, SLOPE_TOTAL = parts_of(2)


def turn(block, shift, axis=1):
    size = block.shape[axis]
    shift = shift % size
    return block if shift == 0 else pltpu.roll(block, shift, axis)


def lanes(rows=8):
    return lax.broadcasted_iota(jnp.int32, (rows, 128), 1)


def pieces_of(block):
    return [block[8 * k : 8 * k + 8] for k in range(block.shape[0] // 8)]


def packed(pieces):
    lane = lanes()
    y, z = (lane >> 4) & 3, lane & 15
    faces = {}
    for dz in (1, -1):
        face = pieces[0]
        for k, piece in enumerate(pieces):
            moved = turn(piece, k - 15 if dz == 1 else k)
            face = moved if k == 0 else jnp.where(z == k, moved, face)
        faces["z", dz] = [face]
    for dy in (1, -1):
        blocks = []
        for first in range(0, len(pieces), 4):
            face = None
            for k, piece in enumerate(pieces[first : first + 4]):
                moved = turn(piece, 16 * k - 48 if dy == 1 else 16 * k)
                face = moved if face is None else jnp.where(y == k, moved, face)
            blocks.append(face)
        faces["y", dy] = blocks
    return faces


def face_start(table, d):
    return table[d][0], table[d][1]


def neighbours(own, landed, table, blank_low, blank_high, put):
    lane = lanes()
    x, y, z = lane >> 6, (lane >> 4) & 3, lane & 15
    count = len(own)

    def column(dx, dy, dz):
        if (dx, dy, dz) == (0, 0, 0):
            return own
        start, rows = table[dx, dy, dz]
        return pieces_of(landed[start : start + rows])

    for ex in (-1, 0, 1):

        def along_x(dy, dz):
            here = column(0, dy, dz)
            if ex == 0:
                return here
            there = column(ex, dy, dz)
            if ex == 1:
                return [turn(jnp.where(x == 0, b, a), 64) for a, b in zip(here, there)]
            return [turn(jnp.where(x == 0, a, b), 64) for a, b in zip(here, there)]

        flat = {dy: along_x(dy, 0) for dy in (-1, 0, 1)}
        deep = {(dy, dz): along_x(dy, dz)[0] for dy in (-1, 0, 1) for dz in (-1, 1)}
        for dy in (-1, 0, 1):
            if blank_low is not None:
                deep[dy, -1] = jnp.where(blank_low, FAR, deep[dy, -1])
                deep[dy, 1] = jnp.where(blank_high, FAR, deep[dy, 1])
        for ey in (-1, 0, 1):
            if ey == 0:
                level = flat[0]
                ends = {dz: deep[0, dz] for dz in (-1, 1)}
            elif ey == 1:
                level = [
                    jnp.where(y == 3, turn(flat[1][k // 4], 48 - 16 * (k % 4)), turn(flat[0][k], -16))
                    for k in range(count)
                ]
                ends = {
                    dz: jnp.where(y == 3, turn(deep[1, dz], 48), turn(deep[0, dz], -16))
                    for dz in (-1, 1)
                }
            else:
                level = [
                    jnp.where(y == 0, turn(flat[-1][k // 4], -16 * (k % 4)), turn(flat[0][k], 16))
                    for k in range(count)
                ]
                ends = {
                    dz: jnp.where(y == 0, turn(deep[-1, dz], -48), turn(deep[0, dz], 16))
                    for dz in (-1, 1)
                }
            put((ex, ey, 0), level)
            put(
                (ex, ey, 1),
                [jnp.where(z == 15, turn(ends[1], 15 - k), turn(level[k], -1)) for k in range(count)],
            )
            put(
                (ex, ey, -1),
                [jnp.where(z == 0, turn(ends[-1], -k), turn(level[k], 1)) for k in range(count)],
            )


def kernel(
    position_ref, velocity_ref, kicks_ref, entry_ref, tally_ref, level_in, fluence_ref,
    position_out, velocity_out, level_out,
    first_ref, rest_ref, heat_ref,
    first, rest, heat, position, velocity, shown, near, near_slope, near_turned, density, force,
    affinity, pos_face, pos_land, slope_face, slope_land, level_ref, handed, choice,
    tile_out, tile_land, laser_out, laser_land, ext, ext_src,
    back_out, back_land, row_out, row_land,
    first_sem, heat_sem, pos_sem, slope_sem, tile_sem, laser_sem, back_sem, row_sem,
):
    gx, gy, gz = (lax.axis_index(a) for a in ("gx", "gy", "gz"))

    def x_place(tx):
        ring = lax.rem(tx + 1, 8)
        return lax.rem(ring, 2), (ring // 2) * 2

    def y_place(ty):
        return lax.rem(ty, 4) * 2, ty // 4

    def device(xp, yp, tz):
        return (xp[0] + yp[0], xp[1] + yp[1], tz)

    ring_place = (gy // 2) * 2 + lax.rem(gx, 2)
    tx = lax.rem(ring_place + 7, 8)
    ty = lax.rem(gy, 2) * 4 + gx // 2
    tz = gz
    xs = {d: x_place(lax.rem(tx + d + 8, 8)) for d in range(-2, 3)}
    ys = {d: y_place(lax.rem(ty + d + 8, 8)) for d in (-1, 0, 1)}
    zs = {d: lax.rem(tz + d + 8, 8) for d in (-1, 0, 1)}

    def partner(d):
        return device(xs[d[0]], ys[d[1]], zs[d[2]])

    my_x, my_y = x_place(gx), y_place(gy)

    def worker(z):
        return device(my_x, my_y, z)

    def owner(z):
        return (tx, ty, z)

    barrier = pltpu.get_barrier_semaphore()
    greeted = [worker(z) for z in range(8)] + [owner(z) for z in range(8)]
    greeted += [partner(d) for d in (WIDE if REACH > 1 else AROUND)]
    for target in greeted:
        pl.semaphore_signal(barrier, inc=1, device_id=target, device_id_type=MESH)

    lane = lanes()
    row = lax.broadcasted_iota(jnp.int32, (8, 128), 0)
    slot = lax.broadcasted_iota(jnp.int32, (16, 128), 0)

    def by_lane(ref, base):
        return jnp.concatenate([ref[pl.ds(base + k, 16, stride=8), :] for k in range(8)], axis=1)

    for c in range(3):
        first_ref[16 * c : 16 * c + 16, :] = by_lane(position_ref, 128 * c)
    tally = jnp.concatenate([tally_ref[k // 4, k % 4 : k % 4 + 1, :] for k in range(8)], axis=1)
    first_ref[48:56, :] = jnp.broadcast_to(tally.astype(F32), (8, 128))
    warm, fluence = jnp.zeros((8, 128), F32), jnp.zeros((8, 128), F32)
    for x in range(4):
        upper = jnp.broadcast_to(level_in[x, :, 0:128], (8, 128))
        lower = jnp.broadcast_to(level_in[x, :, 128:256], (8, 128))
        both = jnp.where(row < 4, upper, lower)
        for k in range(4):
            warm = jnp.where(((row & 3) == k) & ((lane >> 5) == x), turn(both, 32 * x - 32 * k), warm)
        fluence = jnp.where((lane >> 5) == x, fluence_ref[0:1, x : x + 1], fluence)
    heat_ref[:, 0, :] = warm
    heat_ref[:, 1, :] = fluence

    pl.semaphore_wait(barrier, len(greeted))

    def send(src, dst, sems, target):
        pltpu.make_async_remote_copy(
            src_ref=src, dst_ref=dst, send_sem=sems.at[0], recv_sem=sems.at[1],
            device_id=target, device_id_type=MESH,
        ).start()

    def take(ref, sem):
        pltpu.make_async_copy(ref, ref, sem).wait()

    send(first_ref, first, first_sem.at[0], worker(gz))
    for z in range(8):
        send(heat_ref.at[z], heat.at[gz], heat_sem, worker(z))
    for c in range(3):
        rest_ref[16 * c : 16 * c + 16, :] = by_lane(velocity_ref, 128 * c)
    for c in range(6):
        rest_ref[48 + 16 * c : 64 + 16 * c, :] = by_lane(kicks_ref, 128 * c)
    rest_ref[144:160, :] = by_lane(entry_ref, 0).astype(F32)
    send(rest_ref, rest, first_sem.at[1], worker(gz))

    target = lax.broadcasted_iota(jnp.int32, (128, 128), 0)
    source = lax.broadcasted_iota(jnp.int32, (128, 128), 1)
    for k in range(4):
        wanted = (2 * (target >> 6) + k // 2) * 32 + 2 * (target & 15) + k % 2
        choice[128 * k : 128 * k + 128, :] = jnp.where(source == wanted, 1.0, 0.0).astype(F32)

    take(first, first_sem.at[0, 1])
    live = slot.astype(F32) < first[48:49, :]
    live3 = jnp.concatenate([live] * 3, axis=0)
    position[...] = first[0:48, :]
    at_bottom, at_top = tz == 0, tz == 7

    def spread(own, faces, face_ref, land, table, sems):
        at = 0
        places = {}
        for key, blocks in [(("x", 0), own)] + list(faces.items()):
            for k, block in enumerate(blocks):
                face_ref[at + 8 * k : at + 8 * k + 8, :] = block
            places[key] = (at, 8 * len(blocks))
            at += 8 * len(blocks)
        for d in AROUND:
            key = ("z", d[2]) if d[2] else ("y", d[1]) if d[1] else ("x", 0)
            start, rows = places[key]
            there = tuple(-c for c in d)
            send(
                face_ref.at[pl.ds(start, rows)], land.at[pl.ds(table[there][0], rows)],
                sems, partner(d),
            )

    handed[...] = jnp.zeros((16, 128), F32)

    def dynamics(step, carry):
        own = pieces_of(jnp.where(live3, position[...], FAR))
        for k, piece in enumerate(own):
            shown[8 * k : 8 * k + 8, :] = piece
        spread(own, packed(own), pos_face.at[step], pos_land.at[step], POS_ROWS, pos_sem.at[step])
        take(pos_land.at[step], pos_sem.at[step, 1])

        def put_position(e, pieces):
            index = CUBE.index(e)
            for k, piece in enumerate(pieces):
                near[index, 8 * k : 8 * k + 8, :] = piece + float(e[k // 2])

        landed = pos_land[step]
        neighbours(own, landed, POS_ROWS, at_bottom, at_top, put_position)

        def two_densities(i, carry):
            homes = [[shown[pl.ds(16 * c + 2 * i + j, 1), :] for c in range(3)] for j in (0, 1)]
            totals = [jnp.zeros((16, 128), F32) for _ in (0, 1)]
            for index in range(27):
                there = [near[index, 16 * c : 16 * c + 16, :] for c in range(3)]
                for j in (0, 1):
                    d = [there[c] - homes[j][c] for c in range(3)]
                    q = d[0] * d[0] + d[1] * d[1] + d[2] * d[2]
                    w = jnp.maximum(1.0 - q, 0.0)
                    totals[j] = totals[j] + jnp.exp(-2.0 * q) * (w * w)
            for j in (0, 1):
                density[pl.ds(2 * i + j, 1), :] = jnp.sum(totals[j], axis=0, keepdims=True)
            return carry

        lax.fori_loop(0, 8, two_densities, 0)
        rho = jnp.where(live, density[...] - 1.0, 0.0)
        slope = -10.0 * lax.rsqrt(1.0 + jnp.maximum(rho, 0.0))
        density[...] = slope
        own_slope = pieces_of(slope)
        spread(
            own_slope, packed(own_slope), slope_face.at[step], slope_land.at[step], SLOPE_ROWS,
            slope_sem.at[step],
        )

        def two_geometries(i, carry):
            homes = [[shown[pl.ds(16 * c + 2 * i + j, 1), :] for c in range(3)] for j in (0, 1)]
            home_slopes = [density[pl.ds(2 * i + j, 1), :] for j in (0, 1)]
            totals = [[jnp.zeros((16, 128), F32) for _ in range(3)] for _ in (0, 1)]
            for index in range(27):
                there = [near[index, 16 * c : 16 * c + 16, :] for c in range(3)]
                for j in (0, 1):
                    d = [there[c] - homes[j][c] for c in range(3)]
                    q = d[0] * d[0] + d[1] * d[1] + d[2] * d[2]
                    w = jnp.maximum(1.0 - q, 0.0)
                    once = jnp.exp(-q)
                    common = w * (once * once)
                    embed = common * (w + 1.0)
                    affinity[2 * i + j, index] = embed
                    strength = embed * home_slopes[j] + common * once * (3.0 * w + 2.0)
                    totals[j] = [t + strength * c for t, c in zip(totals[j], d)]
            for j in (0, 1):
                for c in range(3):
                    force[pl.ds(16 * c + 2 * i + j, 1), :] = jnp.sum(
                        totals[j][c], axis=0, keepdims=True
                    )
            return carry

        lax.fori_loop(0, 8, two_geometries, 0)

        @pl.when(step == 0)
        def _():
            take(rest, first_sem.at[1, 1])
            take(heat, heat_sem.at[1])
            velocity[...] = rest[0:48, :]
            entry = rest[144:160, :]
            spread_out = lax.dot_general(
                heat[:, 0, :], choice[...], (((1,), (1,)), ((), ())),
                precision=lax.Precision.HIGHEST, preferred_element_type=F32,
            )
            level = jnp.zeros((16, 128), F32)
            for bx, bz, by in itertools.product((0, 1), repeat=3):
                k = 2 * bx + bz
                mine = row == 2 * ((lane >> 4) & 3) + by
                half = jnp.sum(
                    jnp.where(mine, spread_out[:, 128 * k : 128 * k + 128], 0.0), axis=0, keepdims=True
                )
                level = level + jnp.where(entry == float(4 * bx + 2 * by + bz), half, 0.0)
            level_ref[...] = jnp.sqrt(0.06 * level)
            laser_out[...] = heat[:, 1, :]
            for index, d in enumerate(FLAT):
                there = FLAT.index(tuple(-c for c in d))
                send(laser_out, laser_land.at[there], laser_sem, partner(d))

        take(slope_land.at[step], slope_sem.at[step, 1])

        def put_slope(e, pieces):
            index = CUBE.index(e)
            for k, piece in enumerate(pieces):
                near_slope[index, 8 * k : 8 * k + 8, :] = piece
                for c in range(3):
                    at = 16 * c + 8 * k
                    near_turned[index, at : at + 8, :] = piece * near[index, at : at + 8, :]

        neighbours(own_slope, slope_land[step], SLOPE_ROWS, None, None, put_slope)

        def two_forces(i, carry):
            plain = [jnp.zeros((16, 128), F32) for _ in (0, 1)]
            totals = [[jnp.zeros((16, 128), F32) for _ in range(3)] for _ in (0, 1)]
            for index in range(27):
                slopes = near_slope[index]
                turned = [near_turned[index, 16 * c : 16 * c + 16, :] for c in range(3)]
                for j in (0, 1):
                    embed = affinity[2 * i + j, index]
                    plain[j] = plain[j] + embed * slopes
                    totals[j] = [t + embed * c for t, c in zip(totals[j], turned)]
            for j in (0, 1):
                weight = jnp.sum(plain[j], axis=0, keepdims=True)
                for c in range(3):
                    at = pl.ds(16 * c + 2 * i + j, 1)
                    force[at, :] += jnp.sum(totals[j][c], axis=0, keepdims=True) - shown[at, :] * weight
            return carry

        lax.fori_loop(0, 8, two_forces, 0)

        old = velocity[...]
        kicks = rest[pl.ds(pl.multiple_of(48 + 48 * step, 16), 48), :]
        kicked = old + 0.03 * jnp.where(live3, -2.0 * force[...], 0.0)
        noise = jnp.concatenate([level_ref[...]] * 3, axis=0)
        damped = 0.97 * kicked + noise * kicks
        gain = kicked * kicked - damped * damped
        handed[...] += jnp.where(live, 0.5 * (gain[0:16] + gain[16:32] + gain[32:48]), 0.0)
        velocity[...] = jnp.where(live3, damped, old)
        position[...] += 0.03 * jnp.where(live3, damped, 0.0)
        return carry

    lax.fori_loop(0, STEPS, dynamics, 0)

    back_out[0:48, :] = position[...]
    back_out[48:96, :] = velocity[...]

    entry = rest[144:160, :]
    placed = []
    for bx, bz in itertools.product((0, 1), repeat=2):
        low, high = (
            jnp.sum(
                jnp.where(entry == float(4 * bx + 2 * by + bz), handed[...], 0.0), axis=0, keepdims=True
            )
            for by in (0, 1)
        )
        rows_y = jnp.where((row & 1) == 1, high, low)
        placed.append(jnp.where((row >> 1) == ((lane >> 4) & 3), rows_y, 0.0))
    deposit = jnp.dot(
        jnp.concatenate(placed, axis=1), choice[...],
        precision=lax.Precision.HIGHEST, preferred_element_type=F32,
    )

    fold, place = lane >> 6, lane & 63
    depth = (lax.broadcasted_iota(jnp.int32, (24, 128), 1) & 63) + (32 * tz - 16)
    inner_face = (depth >= 0) & (depth < 255)

    def extend(tile_of, put):
        for i in range(FOLD):
            for yt in (-1, 0, 1):
                halves = []
                for h, x in ((0, i - HALO), (1, 3 + HALO - i)):
                    xt, xi = x // 4, x % 4
                    low, mid, high = (
                        turn(tile_of((xt, yt, zt)), 64 * h + 16 + 32 * zt - 32 * xi) for zt in (-1, 0, 1)
                    )
                    halves.append(jnp.where(place < 16, low, jnp.where(place < 48, mid, high)))
                put(i, 8 * yt + 8, jnp.where(fold == 0, halves[0], halves[1]))

    def conduct(t):
        square = 1.0 + t * t
        inverse = pl.reciprocal(square, approx=True)
        return 2.0 - inverse * (2.0 - square * inverse)

    def sweep(start):
        last = ext[start - 1]
        here = ext[start]
        k_here = conduct(here)
        before = (conduct(last) + k_here) * (here - last)
        for i in range(start, FOLD):
            if i < FOLD - 1:
                ahead = ext[i + 1]
                k_ahead = conduct(ahead)
            else:
                ahead, k_ahead = turn(here, 64), turn(k_here, 64)
            after = (k_here + k_ahead) * (ahead - here)
            up_y = (k_here + turn(k_here, -1, 0)) * (turn(here, -1, 0) - here)
            up_z = (k_here + turn(k_here, -1)) * (turn(here, -1) - here)
            up_z = jnp.where(inner_face, up_z, 0.0)
            net = (after - before) + (up_y - turn(up_y, 1, 0)) + (up_z - turn(up_z, 1))
            ext[i] = here + 0.04 * net + ext_src[i]
            before, here, k_here = after, ahead, k_ahead

    def centre():
        tile = None
        for x in range(4):
            h = x // 2
            moved = turn(ext[HALO + (x if h == 0 else 3 - x), 8:16, :], 32 * x - 64 * h - 16)
            tile = moved if tile is None else jnp.where((lane >> 5) == x, moved, tile)
        return tile

    def put_level(i, at, block):
        ext[i, at : at + 8, :] = block

    decay = (lane & 63).astype(F32) + ((32 * tz).astype(F32) - 15.5)
    decay = 0.02 * jnp.exp(decay * (-1.0 / 64.0))

    def put_source(i, at, block):
        ext_src[i, at : at + 8, :] = block * decay

    for turn_of in range(ROUNDS):
        out, land = tile_out.at[turn_of], tile_land.at[turn_of]
        if turn_of == 0:
            out[...] = heat[:, 0, :] + 0.5 * deposit
        else:
            out[...] = centre()
        for index, d in enumerate(WIDE):
            there = WIDE.index(tuple(-c for c in d))
            send(out, land.at[there], tile_sem.at[turn_of], partner(d))
        if turn_of == 0:
            send(back_out, back_land, back_sem, owner(tz))
            take(laser_land, laser_sem.at[1])

            def laser_of(d):
                d = (d[0], d[1], 0)
                return laser_out[...] if d == (0, 0, 0) else laser_land[FLAT.index(d)]

            extend(laser_of, put_source)
        if turn_of == ROUNDS - 1:
            take(back_land, back_sem.at[1])
            for ref, at in ((position_out, 0), (velocity_out, 48)):
                for c in range(3):
                    block = back_land[at + 16 * c : at + 16 * c + 16, :]
                    for k in range(8):
                        ref[pl.ds(128 * c + k, 16, stride=8), :] = block[:, 16 * k : 16 * k + 16]
        take(land, tile_sem.at[turn_of, 1])
        extend(lambda d: out[...] if d == (0, 0, 0) else land[WIDE.index(d)], put_level)
        for start in range(1, HALO + 1):
            sweep(start)

    result = centre()
    for y in range(8):
        row_out[y, :, :] = result[y : y + 1]
        send(row_out.at[y], row_land.at[tz], row_sem, owner(y))

    take(first_ref, first_sem.at[0, 0])
    take(rest_ref, first_sem.at[1, 0])
    take(heat_ref, heat_sem.at[0])
    for step in range(STEPS):
        take(pos_land.at[step], pos_sem.at[step, 0])
        take(slope_land.at[step], slope_sem.at[step, 0])
    take(laser_land, laser_sem.at[0])
    for turn_of in range(ROUNDS):
        take(tile_land.at[turn_of], tile_sem.at[turn_of, 0])
    take(back_out, back_sem.at[0])
    take(row_out, row_sem.at[0])

    take(row_land, row_sem.at[1])
    rows = row_land[:, 0, :]
    for x in range(4):
        line = jnp.zeros((8, 128), F32)
        for k in range(4):
            line = jnp.where(
                ((row & 3) == k) & ((lane >> 5) == k), turn(rows, 32 * k - 32 * x), line
            )
        level_out[x, :, 0:128] = jnp.sum(line[0:4], axis=0, keepdims=True)
        level_out[x, :, 128:256] = jnp.sum(line[4:8], axis=0, keepdims=True)


def face_rows(pieces):
    return 8 * (pieces + 2 + 2 * ((pieces + 3) // 4))


def shards(
    particle_local_offsets,
    particle_velocity,
    stochastic_kicks,
    thermal_mesh_entry,
    occupant_tally,
    fermion_thermal_level,
    fluence_profile,
):
    vmem = pl.BlockSpec(memory_space=pltpu.VMEM)
    buffers = [
        (56, 128), (160, 128), (8, 2, 128),
        (56, 128), (160, 128), (8, 2, 128), (48, 128), (48, 128), (48, 128),
        (27, 48, 128), (27, 16, 128), (27, 48, 128), (16, 128), (48, 128),
        (16, 27, 16, 128), (STEPS, face_rows(6), 128), (STEPS, POS_TOTAL, 128),
        (STEPS, face_rows(2), 128), (STEPS, SLOPE_TOTAL, 128), (16, 128), (16, 128), (512, 128),
        (ROUNDS, 8, 128), (ROUNDS, len(WIDE), 8, 128), (8, 128), (len(FLAT), 8, 128),
        (FOLD, 24, 128), (FOLD, 24, 128),
        (96, 128), (96, 128), (8, 1, 128), (8, 1, 128),
    ]
    sems = [(2, 2), (2,), (STEPS, 2), (STEPS, 2), (ROUNDS, 2), (2,), (2,), (2,)]
    position, velocity, level = pl.pallas_call(
        kernel,
        out_shape=(
            jax.ShapeDtypeStruct((384, 16), F32),
            jax.ShapeDtypeStruct((384, 16), F32),
            jax.ShapeDtypeStruct(fermion_thermal_level.shape, F32),
        ),
        in_specs=[vmem] * 7,
        out_specs=(vmem, vmem, vmem),
        scratch_shapes=[pltpu.VMEM(shape, F32) for shape in buffers]
        + [pltpu.SemaphoreType.DMA(shape) for shape in sems],
        compiler_params=pltpu.CompilerParams(
            collective_id=0, has_side_effects=True, vmem_limit_bytes=32 * 1024 * 1024
        ),
    )(
        particle_local_offsets.reshape(384, 16),
        particle_velocity.reshape(384, 16),
        stochastic_kicks.reshape(768, 16),
        thermal_mesh_entry.reshape(128, 16),
        occupant_tally,
        fermion_thermal_level,
        fluence_profile.T,
    )
    shape = particle_local_offsets.shape
    return position.reshape(shape), velocity.reshape(shape), level


def solution(mesh):
    placed = (
        P(None, None, "gx", "gy", "gz"),
        P(None, None, "gx", "gy", "gz"),
        P(None, None, None, "gx", "gy", "gz"),
        P(None, "gx", "gy", "gz"),
        P("gx", "gy", "gz"),
        P("gx", ("gy", "gz"), None),
        P("gx", ("gy", "gz")),
    )
    return jax.shard_map(
        shards,
        mesh=mesh,
        in_specs=placed,
        out_specs=(
            P(None, None, "gx", "gy", "gz"),
            P(None, None, "gx", "gy", "gz"),
            P("gx", ("gy", "gz"), None),
        ),
        check_vma=False,
    )
```

```python
import itertools

import jax
import jax.numpy as jnp
from jax import lax
from jax.experimental import pallas as pl
from jax.experimental.pallas import tpu as pltpu
from jax.sharding import PartitionSpec as P

MESH = pl.DeviceIdType.MESH
F32 = jnp.float32
STEPS = 2
HALO = 8
ROUNDS = 16 // HALO
REACH = HALO // 4
FAR = 1.0e6
CUBE = [d for d in itertools.product((-1, 0, 1), repeat=3)]
AROUND = sorted((d for d in CUBE if d != (0, 0, 0)), key=lambda d: -sum(map(abs, d)))
WIDE = sorted(
    (
        d
        for d in itertools.product(range(-REACH, REACH + 1), (-1, 0, 1), (-1, 0, 1))
        if d != (0, 0, 0)
    ),
    key=lambda d: -sum(map(abs, d)),
)
FOLD = (4 + 2 * HALO) // 2
FLAT = [d for d in WIDE if d[2] == 0]


def parts_of(pieces):
    rows, start = {}, 0
    for d in AROUND:
        if d[2] != 0:
            count = 8
        elif d[1] != 0:
            count = 8 * ((pieces + 3) // 4)
        else:
            count = 8 * pieces
        rows[d] = (start, count)
        start += count
    return rows, start


POS_ROWS, POS_TOTAL = parts_of(6)
SLOPE_ROWS, SLOPE_TOTAL = parts_of(2)


def turn(block, shift, axis=1):
    size = block.shape[axis]
    shift = shift % size
    return block if shift == 0 else pltpu.roll(block, shift, axis)


def lanes(rows=8):
    return lax.broadcasted_iota(jnp.int32, (rows, 128), 1)


def pieces_of(block):
    return [block[8 * k : 8 * k + 8] for k in range(block.shape[0] // 8)]


def packed(pieces):
    lane = lanes()
    y, z = (lane >> 4) & 3, lane & 15
    faces = {}
    for dz in (1, -1):
        face = pieces[0]
        for k, piece in enumerate(pieces):
            moved = turn(piece, k - 15 if dz == 1 else k)
            face = moved if k == 0 else jnp.where(z == k, moved, face)
        faces["z", dz] = [face]
    for dy in (1, -1):
        blocks = []
        for first in range(0, len(pieces), 4):
            face = None
            for k, piece in enumerate(pieces[first : first + 4]):
                moved = turn(piece, 16 * k - 48 if dy == 1 else 16 * k)
                face = moved if face is None else jnp.where(y == k, moved, face)
            blocks.append(face)
        faces["y", dy] = blocks
    return faces


def face_start(table, d):
    return table[d][0], table[d][1]


def neighbours(own, landed, table, blank_low, blank_high, put):
    lane = lanes()
    x, y, z = lane >> 6, (lane >> 4) & 3, lane & 15
    count = len(own)

    def column(dx, dy, dz):
        if (dx, dy, dz) == (0, 0, 0):
            return own
        start, rows = table[dx, dy, dz]
        return pieces_of(landed[start : start + rows])

    for ex in (-1, 0, 1):

        def along_x(dy, dz):
            here = column(0, dy, dz)
            if ex == 0:
                return here
            there = column(ex, dy, dz)
            if ex == 1:
                return [turn(jnp.where(x == 0, b, a), 64) for a, b in zip(here, there)]
            return [turn(jnp.where(x == 0, a, b), 64) for a, b in zip(here, there)]

        flat = {dy: along_x(dy, 0) for dy in (-1, 0, 1)}
        deep = {(dy, dz): along_x(dy, dz)[0] for dy in (-1, 0, 1) for dz in (-1, 1)}
        for dy in (-1, 0, 1):
            if blank_low is not None:
                deep[dy, -1] = jnp.where(blank_low, FAR, deep[dy, -1])
                deep[dy, 1] = jnp.where(blank_high, FAR, deep[dy, 1])
        for ey in (-1, 0, 1):
            if ey == 0:
                level = flat[0]
                ends = {dz: deep[0, dz] for dz in (-1, 1)}
            elif ey == 1:
                level = [
                    jnp.where(y == 3, turn(flat[1][k // 4], 48 - 16 * (k % 4)), turn(flat[0][k], -16))
                    for k in range(count)
                ]
                ends = {
                    dz: jnp.where(y == 3, turn(deep[1, dz], 48), turn(deep[0, dz], -16))
                    for dz in (-1, 1)
                }
            else:
                level = [
                    jnp.where(y == 0, turn(flat[-1][k // 4], -16 * (k % 4)), turn(flat[0][k], 16))
                    for k in range(count)
                ]
                ends = {
                    dz: jnp.where(y == 0, turn(deep[-1, dz], -48), turn(deep[0, dz], 16))
                    for dz in (-1, 1)
                }
            put((ex, ey, 0), level)
            put(
                (ex, ey, 1),
                [jnp.where(z == 15, turn(ends[1], 15 - k), turn(level[k], -1)) for k in range(count)],
            )
            put(
                (ex, ey, -1),
                [jnp.where(z == 0, turn(ends[-1], -k), turn(level[k], 1)) for k in range(count)],
            )


def kernel(
    position_arg, velocity_arg, kicks_arg, entry_arg, tally_arg, level_arg, fluence_arg,
    position_out, velocity_out, level_out,
    position_ref, velocity_ref, kicks_ref, entry_ref, tally_ref, level_in, fluence_ref,
    first_ref, rest_ref, heat_ref,
    first, rest, heat, position, velocity, shown, near, near_slope, near_turned, density, force,
    affinity, pos_face, pos_land, slope_face, slope_land, level_ref, handed, choice,
    tile_out, tile_land, laser_out, laser_land, ext, ext_src,
    back_out, back_land, row_out, row_land,
    input_sem, first_sem, heat_sem, pos_sem, slope_sem, tile_sem, laser_sem, back_sem, row_sem,
):
    inputs = [
        pltpu.make_async_copy(arg, ref, input_sem.at[k])
        for k, (arg, ref) in enumerate(
            [
                (position_arg, position_ref), (tally_arg, tally_ref), (level_arg, level_in),
                (fluence_arg, fluence_ref), (velocity_arg, velocity_ref), (kicks_arg, kicks_ref),
                (entry_arg, entry_ref),
            ]
        )
    ]
    for copy in inputs:
        copy.start()
    gx, gy, gz = (lax.axis_index(a) for a in ("gx", "gy", "gz"))

    def x_place(tx):
        y = lax.rem(tx + 4, 8)
        return lax.rem(y, 4) * 2, y // 4

    def y_place(ty):
        return lax.rem(ty, 2), (ty // 2) * 2

    def device(xp, yp, tz):
        return (xp[0] + yp[0], xp[1] + yp[1], tz)

    tx = lax.rem(lax.rem(gy, 2) * 4 + gx // 2 + 4, 8)
    ty = (gy // 2) * 2 + lax.rem(gx, 2)
    tz = gz
    xs = {d: x_place(lax.rem(tx + d + 8, 8)) for d in range(-2, 3)}
    ys = {d: y_place(lax.rem(ty + d + 8, 8)) for d in (-1, 0, 1)}
    zs = {d: lax.rem(tz + d + 8, 8) for d in (-1, 0, 1)}

    def partner(d):
        return device(xs[d[0]], ys[d[1]], zs[d[2]])

    my_x, my_y = x_place(gx), y_place(gy)

    def worker(z):
        return device(my_x, my_y, z)

    def owner(z):
        return (tx, ty, z)

    barrier = pltpu.get_barrier_semaphore()
    greeted = [worker(z) for z in range(8)] + [owner(z) for z in range(8)]
    greeted += [partner(d) for d in (WIDE if REACH > 1 else AROUND)]
    for target in greeted:
        pl.semaphore_signal(barrier, inc=1, device_id=target, device_id_type=MESH)

    lane = lanes()
    row = lax.broadcasted_iota(jnp.int32, (8, 128), 0)
    slot = lax.broadcasted_iota(jnp.int32, (16, 128), 0)

    def by_lane(ref, base):
        return jnp.concatenate([ref[pl.ds(base + k, 16, stride=8), :] for k in range(8)], axis=1)

    inputs[0].wait()
    inputs[1].wait()
    for c in range(3):
        first_ref[16 * c : 16 * c + 16, :] = by_lane(position_ref, 128 * c)
    tally = jnp.concatenate([tally_ref[k // 4, k % 4 : k % 4 + 1, :] for k in range(8)], axis=1)
    first_ref[48:56, :] = jnp.broadcast_to(tally.astype(F32), (8, 128))
    pl.semaphore_wait(barrier, len(greeted))

    def send(src, dst, sems, target):
        pltpu.make_async_remote_copy(
            src_ref=src, dst_ref=dst, send_sem=sems.at[0], recv_sem=sems.at[1],
            device_id=target, device_id_type=MESH,
        ).start()

    def take(ref, sem):
        pltpu.make_async_copy(ref, ref, sem).wait()

    send(first_ref, first, first_sem.at[0], worker(gz))
    inputs[2].wait()
    inputs[3].wait()
    warm, fluence = jnp.zeros((8, 128), F32), jnp.zeros((8, 128), F32)
    for x in range(4):
        upper = jnp.broadcast_to(level_in[x, :, 0:128], (8, 128))
        lower = jnp.broadcast_to(level_in[x, :, 128:256], (8, 128))
        both = jnp.where(row < 4, upper, lower)
        for k in range(4):
            warm = jnp.where(((row & 3) == k) & ((lane >> 5) == x), turn(both, 32 * x - 32 * k), warm)
        fluence = jnp.where((lane >> 5) == x, fluence_ref[0:1, x : x + 1], fluence)
    heat_ref[:, 0, :] = warm
    heat_ref[:, 1, :] = fluence
    for z in range(8):
        send(heat_ref.at[z], heat.at[gz], heat_sem, worker(z))
    for copy in inputs[4:]:
        copy.wait()
    for c in range(3):
        rest_ref[16 * c : 16 * c + 16, :] = by_lane(velocity_ref, 128 * c)
    for c in range(6):
        rest_ref[48 + 16 * c : 64 + 16 * c, :] = by_lane(kicks_ref, 128 * c)
    rest_ref[144:160, :] = by_lane(entry_ref, 0).astype(F32)

    target = lax.broadcasted_iota(jnp.int32, (128, 128), 0)
    source = lax.broadcasted_iota(jnp.int32, (128, 128), 1)
    for k in range(4):
        wanted = (2 * (target >> 6) + k // 2) * 32 + 2 * (target & 15) + k % 2
        choice[128 * k : 128 * k + 128, :] = jnp.where(source == wanted, 1.0, 0.0).astype(F32)

    take(first, first_sem.at[0, 1])
    live = slot.astype(F32) < first[48:49, :]
    live3 = jnp.concatenate([live] * 3, axis=0)
    position[...] = first[0:48, :]
    at_bottom, at_top = tz == 0, tz == 7

    def spread(own, faces, face_ref, land, table, sems):
        at = 0
        places = {}
        for key, blocks in [(("x", 0), own)] + list(faces.items()):
            for k, block in enumerate(blocks):
                face_ref[at + 8 * k : at + 8 * k + 8, :] = block
            places[key] = (at, 8 * len(blocks))
            at += 8 * len(blocks)
        for d in AROUND:
            key = ("z", d[2]) if d[2] else ("y", d[1]) if d[1] else ("x", 0)
            start, rows = places[key]
            there = tuple(-c for c in d)
            send(
                face_ref.at[pl.ds(start, rows)], land.at[pl.ds(table[there][0], rows)],
                sems, partner(d),
            )

    handed[...] = jnp.zeros((16, 128), F32)

    def dynamics(step, carry):
        own = pieces_of(jnp.where(live3, position[...], FAR))
        for k, piece in enumerate(own):
            shown[8 * k : 8 * k + 8, :] = piece
        spread(own, packed(own), pos_face.at[step], pos_land.at[step], POS_ROWS, pos_sem.at[step])
        take(pos_land.at[step], pos_sem.at[step, 1])

        @pl.when(step == 0)
        def _():
            send(rest_ref, rest, first_sem.at[1], worker(gz))

        def put_position(e, pieces):
            index = CUBE.index(e)
            for k, piece in enumerate(pieces):
                near[index, 8 * k : 8 * k + 8, :] = piece + float(e[k // 2])

        landed = pos_land[step]
        neighbours(own, landed, POS_ROWS, at_bottom, at_top, put_position)

        def two_densities(i, carry):
            homes = [[shown[pl.ds(16 * c + 2 * i + j, 1), :] for c in range(3)] for j in (0, 1)]
            totals = [jnp.zeros((16, 128), F32) for _ in (0, 1)]
            for index in range(27):
                there = [near[index, 16 * c : 16 * c + 16, :] for c in range(3)]
                for j in (0, 1):
                    d = [there[c] - homes[j][c] for c in range(3)]
                    q = d[0] * d[0] + d[1] * d[1] + d[2] * d[2]
                    w = jnp.maximum(1.0 - q, 0.0)
                    totals[j] = totals[j] + jnp.exp(-2.0 * q) * (w * w)
            for j in (0, 1):
                density[pl.ds(2 * i + j, 1), :] = jnp.sum(totals[j], axis=0, keepdims=True)
            return carry

        lax.fori_loop(0, 8, two_densities, 0)
        rho = jnp.where(live, density[...] - 1.0, 0.0)
        slope = -10.0 * lax.rsqrt(1.0 + jnp.maximum(rho, 0.0))
        density[...] = slope
        own_slope = pieces_of(slope)
        spread(
            own_slope, packed(own_slope), slope_face.at[step], slope_land.at[step], SLOPE_ROWS,
            slope_sem.at[step],
        )

        def two_geometries(i, carry):
            homes = [[shown[pl.ds(16 * c + 2 * i + j, 1), :] for c in range(3)] for j in (0, 1)]
            home_slopes = [density[pl.ds(2 * i + j, 1), :] for j in (0, 1)]
            totals = [[jnp.zeros((16, 128), F32) for _ in range(3)] for _ in (0, 1)]
            for index in range(27):
                there = [near[index, 16 * c : 16 * c + 16, :] for c in range(3)]
                for j in (0, 1):
                    d = [there[c] - homes[j][c] for c in range(3)]
                    q = d[0] * d[0] + d[1] * d[1] + d[2] * d[2]
                    w = jnp.maximum(1.0 - q, 0.0)
                    once = jnp.exp(-q)
                    common = w * (once * once)
                    embed = common * (w + 1.0)
                    affinity[2 * i + j, index] = embed
                    strength = embed * home_slopes[j] + common * once * (3.0 * w + 2.0)
                    totals[j] = [t + strength * c for t, c in zip(totals[j], d)]
            for j in (0, 1):
                for c in range(3):
                    force[pl.ds(16 * c + 2 * i + j, 1), :] = jnp.sum(
                        totals[j][c], axis=0, keepdims=True
                    )
            return carry

        lax.fori_loop(0, 8, two_geometries, 0)

        @pl.when(step == 0)
        def _():
            take(rest, first_sem.at[1, 1])
            take(heat, heat_sem.at[1])
            velocity[...] = rest[0:48, :]
            entry = rest[144:160, :]
            spread_out = lax.dot_general(
                heat[:, 0, :], choice[...], (((1,), (1,)), ((), ())),
                precision=lax.Precision.HIGHEST, preferred_element_type=F32,
            )
            level = jnp.zeros((16, 128), F32)
            for bx, bz, by in itertools.product((0, 1), repeat=3):
                k = 2 * bx + bz
                mine = row == 2 * ((lane >> 4) & 3) + by
                half = jnp.sum(
                    jnp.where(mine, spread_out[:, 128 * k : 128 * k + 128], 0.0), axis=0, keepdims=True
                )
                level = level + jnp.where(entry == float(4 * bx + 2 * by + bz), half, 0.0)
            level_ref[...] = jnp.sqrt(0.06 * level)
            laser_out[...] = heat[:, 1, :]
            for index, d in enumerate(FLAT):
                there = FLAT.index(tuple(-c for c in d))
                send(laser_out, laser_land.at[there], laser_sem, partner(d))

        take(slope_land.at[step], slope_sem.at[step, 1])

        def put_slope(e, pieces):
            index = CUBE.index(e)
            for k, piece in enumerate(pieces):
                near_slope[index, 8 * k : 8 * k + 8, :] = piece
                for c in range(3):
                    at = 16 * c + 8 * k
                    near_turned[index, at : at + 8, :] = piece * near[index, at : at + 8, :]

        neighbours(own_slope, slope_land[step], SLOPE_ROWS, None, None, put_slope)

        def two_forces(i, carry):
            plain = [jnp.zeros((16, 128), F32) for _ in (0, 1)]
            totals = [[jnp.zeros((16, 128), F32) for _ in range(3)] for _ in (0, 1)]
            for index in range(27):
                slopes = near_slope[index]
                turned = [near_turned[index, 16 * c : 16 * c + 16, :] for c in range(3)]
                for j in (0, 1):
                    embed = affinity[2 * i + j, index]
                    plain[j] = plain[j] + embed * slopes
                    totals[j] = [t + embed * c for t, c in zip(totals[j], turned)]
            for j in (0, 1):
                weight = jnp.sum(plain[j], axis=0, keepdims=True)
                for c in range(3):
                    at = pl.ds(16 * c + 2 * i + j, 1)
                    force[at, :] += jnp.sum(totals[j][c], axis=0, keepdims=True) - shown[at, :] * weight
            return carry

        lax.fori_loop(0, 8, two_forces, 0)

        old = velocity[...]
        kicks = rest[pl.ds(pl.multiple_of(48 + 48 * step, 16), 48), :]
        kicked = old + 0.03 * jnp.where(live3, -2.0 * force[...], 0.0)
        noise = jnp.concatenate([level_ref[...]] * 3, axis=0)
        damped = 0.97 * kicked + noise * kicks
        gain = kicked * kicked - damped * damped
        handed[...] += jnp.where(live, 0.5 * (gain[0:16] + gain[16:32] + gain[32:48]), 0.0)
        velocity[...] = jnp.where(live3, damped, old)
        position[...] += 0.03 * jnp.where(live3, damped, 0.0)
        return carry

    lax.fori_loop(0, STEPS, dynamics, 0)

    back_out[0:48, :] = position[...]
    back_out[48:96, :] = velocity[...]

    entry = rest[144:160, :]
    placed = []
    for bx, bz in itertools.product((0, 1), repeat=2):
        low, high = (
            jnp.sum(
                jnp.where(entry == float(4 * bx + 2 * by + bz), handed[...], 0.0), axis=0, keepdims=True
            )
            for by in (0, 1)
        )
        rows_y = jnp.where((row & 1) == 1, high, low)
        placed.append(jnp.where((row >> 1) == ((lane >> 4) & 3), rows_y, 0.0))
    deposit = jnp.dot(
        jnp.concatenate(placed, axis=1), choice[...],
        precision=lax.Precision.HIGHEST, preferred_element_type=F32,
    )

    fold, place = lane >> 6, lane & 63
    depth = (lax.broadcasted_iota(jnp.int32, (24, 128), 1) & 63) + (32 * tz - 16)
    inner_face = (depth >= 0) & (depth < 255)

    def extend(tile_of, put):
        for i in range(FOLD):
            for yt in (-1, 0, 1):
                halves = []
                for h, x in ((0, i - HALO), (1, 3 + HALO - i)):
                    xt, xi = x // 4, x % 4
                    low, mid, high = (
                        turn(tile_of((xt, yt, zt)), 64 * h + 16 + 32 * zt - 32 * xi) for zt in (-1, 0, 1)
                    )
                    halves.append(jnp.where(place < 16, low, jnp.where(place < 48, mid, high)))
                put(i, 8 * yt + 8, jnp.where(fold == 0, halves[0], halves[1]))

    def conduct(t):
        square = 1.0 + t * t
        inverse = pl.reciprocal(square, approx=True)
        return 2.0 - inverse * (2.0 - square * inverse)

    def sweep(start):
        last = ext[start - 1]
        here = ext[start]
        k_here = conduct(here)
        before = (conduct(last) + k_here) * (here - last)
        for i in range(start, FOLD):
            if i < FOLD - 1:
                ahead = ext[i + 1]
                k_ahead = conduct(ahead)
            else:
                ahead, k_ahead = turn(here, 64), turn(k_here, 64)
            after = (k_here + k_ahead) * (ahead - here)
            up_y = (k_here + turn(k_here, -1, 0)) * (turn(here, -1, 0) - here)
            up_z = (k_here + turn(k_here, -1)) * (turn(here, -1) - here)
            up_z = jnp.where(inner_face, up_z, 0.0)
            net = (after - before) + (up_y - turn(up_y, 1, 0)) + (up_z - turn(up_z, 1))
            ext[i] = here + 0.04 * net + ext_src[i]
            before, here, k_here = after, ahead, k_ahead

    def centre():
        tile = None
        for x in range(4):
            h = x // 2
            moved = turn(ext[HALO + (x if h == 0 else 3 - x), 8:16, :], 32 * x - 64 * h - 16)
            tile = moved if tile is None else jnp.where((lane >> 5) == x, moved, tile)
        return tile

    def put_level(i, at, block):
        ext[i, at : at + 8, :] = block

    decay = (lane & 63).astype(F32) + ((32 * tz).astype(F32) - 15.5)
    decay = 0.02 * jnp.exp(decay * (-1.0 / 64.0))

    def put_source(i, at, block):
        ext_src[i, at : at + 8, :] = block * decay

    for turn_of in range(ROUNDS):
        out, land = tile_out.at[turn_of], tile_land.at[turn_of]
        if turn_of == 0:
            out[...] = heat[:, 0, :] + 0.5 * deposit
        else:
            out[...] = centre()
        for index, d in enumerate(WIDE):
            there = WIDE.index(tuple(-c for c in d))
            send(out, land.at[there], tile_sem.at[turn_of], partner(d))
        if turn_of == 0:
            send(back_out, back_land, back_sem, owner(tz))
            take(laser_land, laser_sem.at[1])

            def laser_of(d):
                d = (d[0], d[1], 0)
                return laser_out[...] if d == (0, 0, 0) else laser_land[FLAT.index(d)]

            extend(laser_of, put_source)
        if turn_of == ROUNDS - 1:
            take(back_land, back_sem.at[1])
            for ref, at in ((position_out, 0), (velocity_out, 48)):
                for c in range(3):
                    block = back_land[at + 16 * c : at + 16 * c + 16, :]
                    for k in range(8):
                        ref[pl.ds(128 * c + k, 16, stride=8), :] = block[:, 16 * k : 16 * k + 16]
        take(land, tile_sem.at[turn_of, 1])
        extend(lambda d: out[...] if d == (0, 0, 0) else land[WIDE.index(d)], put_level)
        for start in range(1, HALO + 1):
            sweep(start)

    result = centre()
    for y in range(8):
        row_out[y, :, :] = result[y : y + 1]
        send(row_out.at[y], row_land.at[tz], row_sem, owner(y))

    take(first_ref, first_sem.at[0, 0])
    take(rest_ref, first_sem.at[1, 0])
    take(heat_ref, heat_sem.at[0])
    for step in range(STEPS):
        take(pos_land.at[step], pos_sem.at[step, 0])
        take(slope_land.at[step], slope_sem.at[step, 0])
    take(laser_land, laser_sem.at[0])
    for turn_of in range(ROUNDS):
        take(tile_land.at[turn_of], tile_sem.at[turn_of, 0])
    take(back_out, back_sem.at[0])
    take(row_out, row_sem.at[0])

    take(row_land, row_sem.at[1])
    rows = row_land[:, 0, :]
    for x in range(4):
        line = jnp.zeros((8, 128), F32)
        for k in range(4):
            line = jnp.where(
                ((row & 3) == k) & ((lane >> 5) == k), turn(rows, 32 * k - 32 * x), line
            )
        level_out[x, :, 0:128] = jnp.sum(line[0:4], axis=0, keepdims=True)
        level_out[x, :, 128:256] = jnp.sum(line[4:8], axis=0, keepdims=True)


def face_rows(pieces):
    return 8 * (pieces + 2 + 2 * ((pieces + 3) // 4))


def shards(
    particle_local_offsets,
    particle_velocity,
    stochastic_kicks,
    thermal_mesh_entry,
    occupant_tally,
    fermion_thermal_level,
    fluence_profile,
):
    vmem = pl.BlockSpec(memory_space=pltpu.VMEM)
    args = (
        particle_local_offsets.reshape(384, 16),
        particle_velocity.reshape(384, 16),
        stochastic_kicks.reshape(768, 16),
        thermal_mesh_entry.reshape(128, 16),
        occupant_tally,
        fermion_thermal_level,
        fluence_profile.T,
    )
    buffers = [
        (56, 128), (160, 128), (8, 2, 128),
        (56, 128), (160, 128), (8, 2, 128), (48, 128), (48, 128), (48, 128),
        (27, 48, 128), (27, 16, 128), (27, 48, 128), (16, 128), (48, 128),
        (16, 27, 16, 128), (STEPS, face_rows(6), 128), (STEPS, POS_TOTAL, 128),
        (STEPS, face_rows(2), 128), (STEPS, SLOPE_TOTAL, 128), (16, 128), (16, 128), (512, 128),
        (ROUNDS, 8, 128), (ROUNDS, len(WIDE), 8, 128), (8, 128), (len(FLAT), 8, 128),
        (FOLD, 24, 128), (FOLD, 24, 128),
        (96, 128), (96, 128), (8, 1, 128), (8, 1, 128),
    ]
    sems = [(7,), (2, 2), (2,), (STEPS, 2), (STEPS, 2), (ROUNDS, 2), (2,), (2,), (2,)]
    position, velocity, level = pl.pallas_call(
        kernel,
        out_shape=(
            jax.ShapeDtypeStruct((384, 16), F32),
            jax.ShapeDtypeStruct((384, 16), F32),
            jax.ShapeDtypeStruct(fermion_thermal_level.shape, F32),
        ),
        in_specs=[pl.BlockSpec(memory_space=pltpu.HBM)] * 7,
        out_specs=(vmem, vmem, vmem),
        scratch_shapes=[pltpu.VMEM(arg.shape, arg.dtype) for arg in args]
        + [pltpu.VMEM(shape, F32) for shape in buffers]
        + [pltpu.SemaphoreType.DMA(shape) for shape in sems],
        compiler_params=pltpu.CompilerParams(
            collective_id=0, has_side_effects=True, vmem_limit_bytes=60 * 1024 * 1024
        ),
    )(*args)
    shape = particle_local_offsets.shape
    return position.reshape(shape), velocity.reshape(shape), level


def solution(mesh):
    placed = (
        P(None, None, "gx", "gy", "gz"),
        P(None, None, "gx", "gy", "gz"),
        P(None, None, None, "gx", "gy", "gz"),
        P(None, "gx", "gy", "gz"),
        P("gx", "gy", "gz"),
        P("gx", ("gy", "gz"), None),
        P("gx", ("gy", "gz")),
    )
    return jax.shard_map(
        shards,
        mesh=mesh,
        in_specs=placed,
        out_specs=(
            P(None, None, "gx", "gy", "gz"),
            P(None, None, "gx", "gy", "gz"),
            P("gx", ("gy", "gz"), None),
        ),
        check_vma=False,
    )
```

```python
import itertools
import math

import jax
import jax.numpy as jnp
from jax import lax
from jax.experimental import pallas as pl
from jax.experimental.pallas import tpu as pltpu
from jax.sharding import PartitionSpec as P

MESH = pl.DeviceIdType.MESH
F32 = jnp.float32
STEPS = 2
HALO = 8
ROUNDS = 16 // HALO
REACH = HALO // 4
RANGE = 2.0 * math.log2(math.e)
UNIT = math.sqrt(RANGE)
FAR = 1.0e6
CUBE = [d for d in itertools.product((-1, 0, 1), repeat=3)]
AROUND = sorted((d for d in CUBE if d != (0, 0, 0)), key=lambda d: -sum(map(abs, d)))
WIDE = sorted(
    (
        d
        for d in itertools.product(range(-REACH, REACH + 1), (-1, 0, 1), (-1, 0, 1))
        if d != (0, 0, 0)
    ),
    key=lambda d: -sum(map(abs, d)),
)
FOLD = (4 + 2 * HALO) // 2
FLAT = [d for d in WIDE if d[2] == 0]


def parts_of(pieces):
    rows, start = {}, 0
    for d in AROUND:
        if d[2] != 0:
            count = 8
        elif d[1] != 0:
            count = 8 * ((pieces + 3) // 4)
        else:
            count = 8 * pieces
        rows[d] = (start, count)
        start += count
    return rows, start


POS_ROWS, POS_TOTAL = parts_of(6)
SLOPE_ROWS, SLOPE_TOTAL = parts_of(2)


def turn(block, shift, axis=1):
    size = block.shape[axis]
    shift = shift % size
    return block if shift == 0 else pltpu.roll(block, shift, axis)


def lanes(rows=8):
    return lax.broadcasted_iota(jnp.int32, (rows, 128), 1)


def pieces_of(block):
    return [block[8 * k : 8 * k + 8] for k in range(block.shape[0] // 8)]


def packed(pieces):
    lane = lanes()
    y, z = (lane >> 4) & 3, lane & 15
    faces = {}
    for dz in (1, -1):
        face = pieces[0]
        for k, piece in enumerate(pieces):
            moved = turn(piece, k - 15 if dz == 1 else k)
            face = moved if k == 0 else jnp.where(z == k, moved, face)
        faces["z", dz] = [face]
    for dy in (1, -1):
        blocks = []
        for first in range(0, len(pieces), 4):
            face = None
            for k, piece in enumerate(pieces[first : first + 4]):
                moved = turn(piece, 16 * k - 48 if dy == 1 else 16 * k)
                face = moved if face is None else jnp.where(y == k, moved, face)
            blocks.append(face)
        faces["y", dy] = blocks
    return faces


def face_start(table, d):
    return table[d][0], table[d][1]


def neighbours(own, landed, table, blank_low, blank_high, put):
    lane = lanes()
    x, y, z = lane >> 6, (lane >> 4) & 3, lane & 15
    count = len(own)

    def column(dx, dy, dz):
        if (dx, dy, dz) == (0, 0, 0):
            return own
        start, rows = table[dx, dy, dz]
        return pieces_of(landed[start : start + rows])

    for ex in (-1, 0, 1):

        def along_x(dy, dz):
            here = column(0, dy, dz)
            if ex == 0:
                return here
            there = column(ex, dy, dz)
            if ex == 1:
                return [turn(jnp.where(x == 0, b, a), 64) for a, b in zip(here, there)]
            return [turn(jnp.where(x == 0, a, b), 64) for a, b in zip(here, there)]

        flat = {dy: along_x(dy, 0) for dy in (-1, 0, 1)}
        deep = {(dy, dz): along_x(dy, dz)[0] for dy in (-1, 0, 1) for dz in (-1, 1)}
        for dy in (-1, 0, 1):
            if blank_low is not None:
                deep[dy, -1] = jnp.where(blank_low, FAR, deep[dy, -1])
                deep[dy, 1] = jnp.where(blank_high, FAR, deep[dy, 1])
        for ey in (-1, 0, 1):
            if ey == 0:
                level = flat[0]
                ends = {dz: deep[0, dz] for dz in (-1, 1)}
            elif ey == 1:
                level = [
                    jnp.where(y == 3, turn(flat[1][k // 4], 48 - 16 * (k % 4)), turn(flat[0][k], -16))
                    for k in range(count)
                ]
                ends = {
                    dz: jnp.where(y == 3, turn(deep[1, dz], 48), turn(deep[0, dz], -16))
                    for dz in (-1, 1)
                }
            else:
                level = [
                    jnp.where(y == 0, turn(flat[-1][k // 4], -16 * (k % 4)), turn(flat[0][k], 16))
                    for k in range(count)
                ]
                ends = {
                    dz: jnp.where(y == 0, turn(deep[-1, dz], -48), turn(deep[0, dz], 16))
                    for dz in (-1, 1)
                }
            put((ex, ey, 0), level)
            put(
                (ex, ey, 1),
                [jnp.where(z == 15, turn(ends[1], 15 - k), turn(level[k], -1)) for k in range(count)],
            )
            put(
                (ex, ey, -1),
                [jnp.where(z == 0, turn(ends[-1], -k), turn(level[k], 1)) for k in range(count)],
            )


def kernel(
    position_arg, velocity_arg, kicks_arg, entry_arg, tally_arg, level_arg, fluence_arg,
    position_out, velocity_out, level_out,
    position_ref, velocity_ref, kicks_ref, entry_ref, tally_ref, level_in, fluence_ref,
    first_ref, rest_ref, heat_ref,
    first, rest, heat, position, velocity, shown, near, near_slope, near_turned, density, force,
    affinity, pos_face, pos_land, slope_face, slope_land, level_ref, handed, choice,
    tile_out, tile_land, laser_out, laser_land, ext, ext_src,
    back_out, back_land, row_out, row_land,
    input_sem, first_sem, heat_sem, pos_sem, slope_sem, tile_sem, laser_sem, back_sem, row_sem,
):
    inputs = [
        pltpu.make_async_copy(arg, ref, input_sem.at[k])
        for k, (arg, ref) in enumerate(
            [
                (position_arg, position_ref), (tally_arg, tally_ref), (level_arg, level_in),
                (fluence_arg, fluence_ref), (velocity_arg, velocity_ref), (kicks_arg, kicks_ref),
                (entry_arg, entry_ref),
            ]
        )
    ]
    for copy in inputs:
        copy.start()
    gx, gy, gz = (lax.axis_index(a) for a in ("gx", "gy", "gz"))

    def x_place(tx):
        y = lax.rem(tx + 4, 8)
        return lax.rem(y, 4) * 2, y // 4

    def y_place(ty):
        return lax.rem(ty, 2), (ty // 2) * 2

    def device(xp, yp, tz):
        return (xp[0] + yp[0], xp[1] + yp[1], tz)

    tx = lax.rem(lax.rem(gy, 2) * 4 + gx // 2 + 4, 8)
    ty = (gy // 2) * 2 + lax.rem(gx, 2)
    tz = gz
    xs = {d: x_place(lax.rem(tx + d + 8, 8)) for d in range(-2, 3)}
    ys = {d: y_place(lax.rem(ty + d + 8, 8)) for d in (-1, 0, 1)}
    zs = {d: lax.rem(tz + d + 8, 8) for d in (-1, 0, 1)}

    def partner(d):
        return device(xs[d[0]], ys[d[1]], zs[d[2]])

    my_x, my_y = x_place(gx), y_place(gy)

    def worker(z):
        return device(my_x, my_y, z)

    def owner(z):
        return (tx, ty, z)

    barrier = pltpu.get_barrier_semaphore()
    greeted = [worker(z) for z in range(8)] + [owner(z) for z in range(8)]
    greeted += [partner(d) for d in (WIDE if REACH > 1 else AROUND)]
    for target in greeted:
        pl.semaphore_signal(barrier, inc=1, device_id=target, device_id_type=MESH)

    lane = lanes()
    row = lax.broadcasted_iota(jnp.int32, (8, 128), 0)
    slot = lax.broadcasted_iota(jnp.int32, (16, 128), 0)

    def by_lane(ref, base):
        return jnp.concatenate([ref[pl.ds(base + k, 16, stride=8), :] for k in range(8)], axis=1)

    inputs[0].wait()
    inputs[1].wait()
    for c in range(3):
        first_ref[16 * c : 16 * c + 16, :] = by_lane(position_ref, 128 * c)
    tally = jnp.concatenate([tally_ref[k // 4, k % 4 : k % 4 + 1, :] for k in range(8)], axis=1)
    first_ref[48:56, :] = jnp.broadcast_to(tally.astype(F32), (8, 128))
    pl.semaphore_wait(barrier, len(greeted))

    def send(src, dst, sems, target):
        pltpu.make_async_remote_copy(
            src_ref=src, dst_ref=dst, send_sem=sems.at[0], recv_sem=sems.at[1],
            device_id=target, device_id_type=MESH,
        ).start()

    def take(ref, sem):
        pltpu.make_async_copy(ref, ref, sem).wait()

    send(first_ref, first, first_sem.at[0], worker(gz))
    inputs[2].wait()
    inputs[3].wait()
    warm, fluence = jnp.zeros((8, 128), F32), jnp.zeros((8, 128), F32)
    for x in range(4):
        upper = jnp.broadcast_to(level_in[x, :, 0:128], (8, 128))
        lower = jnp.broadcast_to(level_in[x, :, 128:256], (8, 128))
        both = jnp.where(row < 4, upper, lower)
        for k in range(4):
            warm = jnp.where(((row & 3) == k) & ((lane >> 5) == x), turn(both, 32 * x - 32 * k), warm)
        fluence = jnp.where((lane >> 5) == x, fluence_ref[0:1, x : x + 1], fluence)
    heat_ref[:, 0, :] = warm
    heat_ref[:, 1, :] = fluence
    for z in range(8):
        send(heat_ref.at[z], heat.at[gz], heat_sem, worker(z))
    for copy in inputs[4:]:
        copy.wait()
    for c in range(3):
        rest_ref[16 * c : 16 * c + 16, :] = by_lane(velocity_ref, 128 * c)
    for c in range(6):
        rest_ref[48 + 16 * c : 64 + 16 * c, :] = by_lane(kicks_ref, 128 * c)
    rest_ref[144:160, :] = by_lane(entry_ref, 0).astype(F32)

    target = lax.broadcasted_iota(jnp.int32, (128, 128), 0)
    source = lax.broadcasted_iota(jnp.int32, (128, 128), 1)
    for k in range(4):
        wanted = (2 * (target >> 6) + k // 2) * 32 + 2 * (target & 15) + k % 2
        choice[128 * k : 128 * k + 128, :] = jnp.where(source == wanted, 1.0, 0.0).astype(F32)

    take(first, first_sem.at[0, 1])
    live = slot.astype(F32) < first[48:49, :]
    live3 = jnp.concatenate([live] * 3, axis=0)
    position[...] = first[0:48, :]
    at_bottom, at_top = tz == 0, tz == 7

    def spread(own, faces, face_ref, land, table, sems):
        at = 0
        places = {}
        for key, blocks in [(("x", 0), own)] + list(faces.items()):
            for k, block in enumerate(blocks):
                face_ref[at + 8 * k : at + 8 * k + 8, :] = block
            places[key] = (at, 8 * len(blocks))
            at += 8 * len(blocks)
        for d in AROUND:
            key = ("z", d[2]) if d[2] else ("y", d[1]) if d[1] else ("x", 0)
            start, rows = places[key]
            there = tuple(-c for c in d)
            send(
                face_ref.at[pl.ds(start, rows)], land.at[pl.ds(table[there][0], rows)],
                sems, partner(d),
            )

    handed[...] = jnp.zeros((16, 128), F32)

    def dynamics(step, carry):
        own = pieces_of(jnp.where(live3, UNIT * position[...], FAR))
        for k, piece in enumerate(own):
            shown[8 * k : 8 * k + 8, :] = piece
        spread(own, packed(own), pos_face.at[step], pos_land.at[step], POS_ROWS, pos_sem.at[step])
        take(pos_land.at[step], pos_sem.at[step, 1])

        @pl.when(step == 0)
        def _():
            send(rest_ref, rest, first_sem.at[1], worker(gz))

        def put_position(e, pieces):
            index = CUBE.index(e)
            for k, piece in enumerate(pieces):
                near[index, 8 * k : 8 * k + 8, :] = piece + UNIT * e[k // 2]

        landed = pos_land[step]
        neighbours(own, landed, POS_ROWS, at_bottom, at_top, put_position)

        def two_densities(i, carry):
            homes = [[shown[pl.ds(16 * c + 2 * i + j, 1), :] for c in range(3)] for j in (0, 1)]
            totals = [jnp.zeros((16, 128), F32) for _ in (0, 1)]
            for index in range(27):
                there = [near[index, 16 * c : 16 * c + 16, :] for c in range(3)]
                for j in (0, 1):
                    d = [there[c] - homes[j][c] for c in range(3)]
                    q = d[0] * d[0] + d[1] * d[1] + d[2] * d[2]
                    left = RANGE - q
                    w = jnp.maximum(left, 0.0)
                    totals[j] = totals[j] + jnp.exp2(left) * (w * w)
            for j in (0, 1):
                density[pl.ds(2 * i + j, 1), :] = jnp.sum(totals[j], axis=0, keepdims=True)
            return carry

        lax.fori_loop(0, 8, two_densities, 0)
        rho = jnp.where(live, math.exp(-2.0) / RANGE**2 * density[...] - 1.0, 0.0)
        slope = -10.0 * lax.rsqrt(1.0 + jnp.maximum(rho, 0.0))
        density[...] = slope
        own_slope = pieces_of(slope)
        spread(
            own_slope, packed(own_slope), slope_face.at[step], slope_land.at[step], SLOPE_ROWS,
            slope_sem.at[step],
        )

        def two_geometries(i, carry):
            homes = [[shown[pl.ds(16 * c + 2 * i + j, 1), :] for c in range(3)] for j in (0, 1)]
            home_slopes = [density[pl.ds(2 * i + j, 1), :] for j in (0, 1)]
            totals = [[jnp.zeros((16, 128), F32) for _ in range(3)] for _ in (0, 1)]
            for index in range(27):
                there = [near[index, 16 * c : 16 * c + 16, :] for c in range(3)]
                for j in (0, 1):
                    d = [there[c] - homes[j][c] for c in range(3)]
                    q = d[0] * d[0] + d[1] * d[1] + d[2] * d[2]
                    w = jnp.maximum(RANGE - q, 0.0) * (1.0 / RANGE)
                    once = jnp.exp2(-0.5 * q)
                    common = w * (once * once)
                    embed = common * (w + 1.0)
                    affinity[2 * i + j, index] = embed
                    strength = embed * home_slopes[j] + common * once * (3.0 * w + 2.0)
                    totals[j] = [t + strength * c for t, c in zip(totals[j], d)]
            for j in (0, 1):
                for c in range(3):
                    force[pl.ds(16 * c + 2 * i + j, 1), :] = jnp.sum(
                        totals[j][c], axis=0, keepdims=True
                    )
            return carry

        lax.fori_loop(0, 8, two_geometries, 0)

        @pl.when(step == 0)
        def _():
            take(rest, first_sem.at[1, 1])
            take(heat, heat_sem.at[1])
            velocity[...] = rest[0:48, :]
            entry = rest[144:160, :]
            spread_out = lax.dot_general(
                heat[:, 0, :], choice[...], (((1,), (1,)), ((), ())),
                precision=lax.Precision.HIGHEST, preferred_element_type=F32,
            )
            level = jnp.zeros((16, 128), F32)
            for bx, bz, by in itertools.product((0, 1), repeat=3):
                k = 2 * bx + bz
                mine = row == 2 * ((lane >> 4) & 3) + by
                half = jnp.sum(
                    jnp.where(mine, spread_out[:, 128 * k : 128 * k + 128], 0.0), axis=0, keepdims=True
                )
                level = level + jnp.where(entry == float(4 * bx + 2 * by + bz), half, 0.0)
            level_ref[...] = jnp.sqrt(0.06 * level)
            laser_out[...] = heat[:, 1, :]
            for index, d in enumerate(FLAT):
                there = FLAT.index(tuple(-c for c in d))
                send(laser_out, laser_land.at[there], laser_sem, partner(d))

        take(slope_land.at[step], slope_sem.at[step, 1])

        def put_slope(e, pieces):
            index = CUBE.index(e)
            for k, piece in enumerate(pieces):
                near_slope[index, 8 * k : 8 * k + 8, :] = piece
                for c in range(3):
                    at = 16 * c + 8 * k
                    near_turned[index, at : at + 8, :] = piece * near[index, at : at + 8, :]

        neighbours(own_slope, slope_land[step], SLOPE_ROWS, None, None, put_slope)

        def two_forces(i, carry):
            plain = [jnp.zeros((16, 128), F32) for _ in (0, 1)]
            totals = [[jnp.zeros((16, 128), F32) for _ in range(3)] for _ in (0, 1)]
            for index in range(27):
                slopes = near_slope[index]
                turned = [near_turned[index, 16 * c : 16 * c + 16, :] for c in range(3)]
                for j in (0, 1):
                    embed = affinity[2 * i + j, index]
                    plain[j] = plain[j] + embed * slopes
                    totals[j] = [t + embed * c for t, c in zip(totals[j], turned)]
            for j in (0, 1):
                weight = jnp.sum(plain[j], axis=0, keepdims=True)
                for c in range(3):
                    at = pl.ds(16 * c + 2 * i + j, 1)
                    force[at, :] += jnp.sum(totals[j][c], axis=0, keepdims=True) - shown[at, :] * weight
            return carry

        lax.fori_loop(0, 8, two_forces, 0)

        old = velocity[...]
        kicks = rest[pl.ds(pl.multiple_of(48 + 48 * step, 16), 48), :]
        kicked = old + 0.03 * jnp.where(live3, (-2.0 / UNIT) * force[...], 0.0)
        noise = jnp.concatenate([level_ref[...]] * 3, axis=0)
        damped = 0.97 * kicked + noise * kicks
        gain = kicked * kicked - damped * damped
        handed[...] += jnp.where(live, 0.5 * (gain[0:16] + gain[16:32] + gain[32:48]), 0.0)
        velocity[...] = jnp.where(live3, damped, old)
        position[...] += 0.03 * jnp.where(live3, damped, 0.0)
        return carry

    lax.fori_loop(0, STEPS, dynamics, 0)

    back_out[0:48, :] = position[...]
    back_out[48:96, :] = velocity[...]

    entry = rest[144:160, :]
    placed = []
    for bx, bz in itertools.product((0, 1), repeat=2):
        low, high = (
            jnp.sum(
                jnp.where(entry == float(4 * bx + 2 * by + bz), handed[...], 0.0), axis=0, keepdims=True
            )
            for by in (0, 1)
        )
        rows_y = jnp.where((row & 1) == 1, high, low)
        placed.append(jnp.where((row >> 1) == ((lane >> 4) & 3), rows_y, 0.0))
    deposit = jnp.dot(
        jnp.concatenate(placed, axis=1), choice[...],
        precision=lax.Precision.HIGHEST, preferred_element_type=F32,
    )

    fold, place = lane >> 6, lane & 63
    depth = (lax.broadcasted_iota(jnp.int32, (24, 128), 1) & 63) + (32 * tz - 16)
    inner_face = (depth >= 0) & (depth < 255)

    def extend(tile_of, put):
        for i in range(FOLD):
            for yt in (-1, 0, 1):
                halves = []
                for h, x in ((0, i - HALO), (1, 3 + HALO - i)):
                    xt, xi = x // 4, x % 4
                    low, mid, high = (
                        turn(tile_of((xt, yt, zt)), 64 * h + 16 + 32 * zt - 32 * xi) for zt in (-1, 0, 1)
                    )
                    halves.append(jnp.where(place < 16, low, jnp.where(place < 48, mid, high)))
                put(i, 8 * yt + 8, jnp.where(fold == 0, halves[0], halves[1]))

    def conduct(t):
        square = 1.0 + t * t
        inverse = pl.reciprocal(square, approx=True)
        return 2.0 - inverse * (2.0 - square * inverse)

    def sweep(start):
        last = ext[start - 1]
        here = ext[start]
        k_here = conduct(here)
        before = (conduct(last) + k_here) * (here - last)
        for i in range(start, FOLD):
            if i < FOLD - 1:
                ahead = ext[i + 1]
                k_ahead = conduct(ahead)
            else:
                ahead, k_ahead = turn(here, 64), turn(k_here, 64)
            after = (k_here + k_ahead) * (ahead - here)
            up_y = (k_here + turn(k_here, -1, 0)) * (turn(here, -1, 0) - here)
            up_z = (k_here + turn(k_here, -1)) * (turn(here, -1) - here)
            up_z = jnp.where(inner_face, up_z, 0.0)
            net = (after - before) + (up_y - turn(up_y, 1, 0)) + (up_z - turn(up_z, 1))
            ext[i] = here + 0.04 * net + ext_src[i]
            before, here, k_here = after, ahead, k_ahead

    def centre():
        tile = None
        for x in range(4):
            h = x // 2
            moved = turn(ext[HALO + (x if h == 0 else 3 - x), 8:16, :], 32 * x - 64 * h - 16)
            tile = moved if tile is None else jnp.where((lane >> 5) == x, moved, tile)
        return tile

    def put_level(i, at, block):
        ext[i, at : at + 8, :] = block

    decay = (lane & 63).astype(F32) + ((32 * tz).astype(F32) - 15.5)
    decay = 0.02 * jnp.exp(decay * (-1.0 / 64.0))

    def put_source(i, at, block):
        ext_src[i, at : at + 8, :] = block * decay

    for turn_of in range(ROUNDS):
        out, land = tile_out.at[turn_of], tile_land.at[turn_of]
        if turn_of == 0:
            out[...] = heat[:, 0, :] + 0.5 * deposit
        else:
            out[...] = centre()
        for index, d in enumerate(WIDE):
            there = WIDE.index(tuple(-c for c in d))
            send(out, land.at[there], tile_sem.at[turn_of], partner(d))
        if turn_of == 0:
            send(back_out, back_land, back_sem, owner(tz))
            take(laser_land, laser_sem.at[1])

            def laser_of(d):
                d = (d[0], d[1], 0)
                return laser_out[...] if d == (0, 0, 0) else laser_land[FLAT.index(d)]

            extend(laser_of, put_source)
        if turn_of == ROUNDS - 1:
            take(back_land, back_sem.at[1])
            for ref, at in ((position_out, 0), (velocity_out, 48)):
                for c in range(3):
                    block = back_land[at + 16 * c : at + 16 * c + 16, :]
                    for k in range(8):
                        ref[pl.ds(128 * c + k, 16, stride=8), :] = block[:, 16 * k : 16 * k + 16]
        take(land, tile_sem.at[turn_of, 1])
        extend(lambda d: out[...] if d == (0, 0, 0) else land[WIDE.index(d)], put_level)
        for start in range(1, HALO + 1):
            sweep(start)

    result = centre()
    for y in range(8):
        row_out[y, :, :] = result[y : y + 1]
        send(row_out.at[y], row_land.at[tz], row_sem, owner(y))

    take(first_ref, first_sem.at[0, 0])
    take(rest_ref, first_sem.at[1, 0])
    take(heat_ref, heat_sem.at[0])
    for step in range(STEPS):
        take(pos_land.at[step], pos_sem.at[step, 0])
        take(slope_land.at[step], slope_sem.at[step, 0])
    take(laser_land, laser_sem.at[0])
    for turn_of in range(ROUNDS):
        take(tile_land.at[turn_of], tile_sem.at[turn_of, 0])
    take(back_out, back_sem.at[0])
    take(row_out, row_sem.at[0])

    take(row_land, row_sem.at[1])
    rows = row_land[:, 0, :]
    for x in range(4):
        line = jnp.zeros((8, 128), F32)
        for k in range(4):
            line = jnp.where(
                ((row & 3) == k) & ((lane >> 5) == k), turn(rows, 32 * k - 32 * x), line
            )
        level_out[x, :, 0:128] = jnp.sum(line[0:4], axis=0, keepdims=True)
        level_out[x, :, 128:256] = jnp.sum(line[4:8], axis=0, keepdims=True)


def deliver(*refs):
    sources, results, stops, sem = refs[:3], refs[3:6], refs[6:9], refs[9]
    copies = [
        [pltpu.make_async_copy(src, dst, sem.at[leg, k]) for k, (src, dst) in enumerate(pairs)]
        for leg, pairs in enumerate((zip(sources, stops), zip(stops, results)))
    ]
    for copy in copies[0]:
        copy.start()
    for copy, onward in zip(*copies):
        copy.wait()
        onward.start()
    for copy in copies[1]:
        copy.wait()


def face_rows(pieces):
    return 8 * (pieces + 2 + 2 * ((pieces + 3) // 4))


def shards(
    particle_local_offsets,
    particle_velocity,
    stochastic_kicks,
    thermal_mesh_entry,
    occupant_tally,
    fermion_thermal_level,
    fluence_profile,
):
    vmem = pl.BlockSpec(memory_space=pltpu.VMEM)
    args = (
        particle_local_offsets.reshape(384, 16),
        particle_velocity.reshape(384, 16),
        stochastic_kicks.reshape(768, 16),
        thermal_mesh_entry.reshape(128, 16),
        occupant_tally,
        fermion_thermal_level,
        fluence_profile.T,
    )
    buffers = [
        (56, 128), (160, 128), (8, 2, 128),
        (56, 128), (160, 128), (8, 2, 128), (48, 128), (48, 128), (48, 128),
        (27, 48, 128), (27, 16, 128), (27, 48, 128), (16, 128), (48, 128),
        (16, 27, 16, 128), (STEPS, face_rows(6), 128), (STEPS, POS_TOTAL, 128),
        (STEPS, face_rows(2), 128), (STEPS, SLOPE_TOTAL, 128), (16, 128), (16, 128), (512, 128),
        (ROUNDS, 8, 128), (ROUNDS, len(WIDE), 8, 128), (8, 128), (len(FLAT), 8, 128),
        (FOLD, 24, 128), (FOLD, 24, 128),
        (96, 128), (96, 128), (8, 1, 128), (8, 1, 128),
    ]
    sems = [(7,), (2, 2), (2,), (STEPS, 2), (STEPS, 2), (ROUNDS, 2), (2,), (2,), (2,)]
    position, velocity, level = pl.pallas_call(
        kernel,
        out_shape=(
            jax.ShapeDtypeStruct((384, 16), F32),
            jax.ShapeDtypeStruct((384, 16), F32),
            jax.ShapeDtypeStruct(fermion_thermal_level.shape, F32),
        ),
        in_specs=[pl.BlockSpec(memory_space=pltpu.HBM)] * 7,
        out_specs=(vmem, vmem, vmem),
        scratch_shapes=[pltpu.VMEM(arg.shape, arg.dtype) for arg in args]
        + [pltpu.VMEM(shape, F32) for shape in buffers]
        + [pltpu.SemaphoreType.DMA(shape) for shape in sems],
        compiler_params=pltpu.CompilerParams(
            collective_id=0, has_side_effects=True, vmem_limit_bytes=60 * 1024 * 1024
        ),
    )(*args)
    results = (position, velocity, level)
    position, velocity, level = pl.pallas_call(
        deliver,
        out_shape=tuple(jax.ShapeDtypeStruct(result.shape, F32) for result in results),
        in_specs=[pl.BlockSpec(memory_space=pltpu.HBM)] * 3,
        out_specs=(pl.BlockSpec(memory_space=pltpu.HBM),) * 3,
        scratch_shapes=[pltpu.VMEM(result.shape, F32) for result in results]
        + [pltpu.SemaphoreType.DMA((2, 3))],
        compiler_params=pltpu.CompilerParams(vmem_limit_bytes=60 * 1024 * 1024),
    )(*results)
    shape = particle_local_offsets.shape
    return position.reshape(shape), velocity.reshape(shape), level


def solution(mesh):
    placed = (
        P(None, None, "gx", "gy", "gz"),
        P(None, None, "gx", "gy", "gz"),
        P(None, None, None, "gx", "gy", "gz"),
        P(None, "gx", "gy", "gz"),
        P("gx", "gy", "gz"),
        P("gx", ("gy", "gz"), None),
        P("gx", ("gy", "gz")),
    )
    return jax.shard_map(
        shards,
        mesh=mesh,
        in_specs=placed,
        out_specs=(
            P(None, None, "gx", "gy", "gz"),
            P(None, None, "gx", "gy", "gz"),
            P("gx", ("gy", "gz"), None),
        ),
        check_vma=False,
    )
```

```python
import itertools
import math

import jax
import jax.numpy as jnp
from jax import lax
from jax.experimental import pallas as pl
from jax.experimental.pallas import tpu as pltpu
from jax.sharding import PartitionSpec as P

MESH = pl.DeviceIdType.MESH
F32 = jnp.float32
STEPS = 2
HALO = 8
ROUNDS = 16 // HALO
REACH = HALO // 4
RANGE = 2.0 * math.log2(math.e)
UNIT = math.sqrt(RANGE)
FAR = 1.0e6
CUBE = [d for d in itertools.product((-1, 0, 1), repeat=3)]
AROUND = sorted((d for d in CUBE if d != (0, 0, 0)), key=lambda d: -sum(map(abs, d)))
WIDE = sorted(
    (
        d
        for d in itertools.product(range(-REACH, REACH + 1), (-1, 0, 1), (-1, 0, 1))
        if d != (0, 0, 0)
    ),
    key=lambda d: -sum(map(abs, d)),
)
FOLD = (4 + 2 * HALO) // 2
FLAT = [d for d in WIDE if d[2] == 0]


def parts_of(pieces):
    rows, start = {}, 0
    for d in AROUND:
        if d[2] != 0:
            count = 8
        elif d[1] != 0:
            count = 8 * ((pieces + 3) // 4)
        else:
            count = 8 * pieces
        rows[d] = (start, count)
        start += count
    return rows, start


POS_ROWS, POS_TOTAL = parts_of(6)
SLOPE_ROWS, SLOPE_TOTAL = parts_of(2)


def turn(block, shift, axis=1):
    size = block.shape[axis]
    shift = shift % size
    return block if shift == 0 else pltpu.roll(block, shift, axis)


def lanes(rows=8):
    return lax.broadcasted_iota(jnp.int32, (rows, 128), 1)


def pieces_of(block):
    return [block[8 * k : 8 * k + 8] for k in range(block.shape[0] // 8)]


def packed(pieces):
    lane = lanes()
    y, z = (lane >> 4) & 3, lane & 15
    faces = {}
    for dz in (1, -1):
        face = pieces[0]
        for k, piece in enumerate(pieces):
            moved = turn(piece, k - 15 if dz == 1 else k)
            face = moved if k == 0 else jnp.where(z == k, moved, face)
        faces["z", dz] = [face]
    for dy in (1, -1):
        blocks = []
        for first in range(0, len(pieces), 4):
            face = None
            for k, piece in enumerate(pieces[first : first + 4]):
                moved = turn(piece, 16 * k - 48 if dy == 1 else 16 * k)
                face = moved if face is None else jnp.where(y == k, moved, face)
            blocks.append(face)
        faces["y", dy] = blocks
    return faces


def face_start(table, d):
    return table[d][0], table[d][1]


def neighbours(own, landed, table, blank_low, blank_high, put):
    lane = lanes()
    x, y, z = lane >> 6, (lane >> 4) & 3, lane & 15
    count = len(own)

    def column(dx, dy, dz):
        if (dx, dy, dz) == (0, 0, 0):
            return own
        start, rows = table[dx, dy, dz]
        return pieces_of(landed[start : start + rows])

    for ex in (-1, 0, 1):

        def along_x(dy, dz):
            here = column(0, dy, dz)
            if ex == 0:
                return here
            there = column(ex, dy, dz)
            if ex == 1:
                return [turn(jnp.where(x == 0, b, a), 64) for a, b in zip(here, there)]
            return [turn(jnp.where(x == 0, a, b), 64) for a, b in zip(here, there)]

        flat = {dy: along_x(dy, 0) for dy in (-1, 0, 1)}
        deep = {(dy, dz): along_x(dy, dz)[0] for dy in (-1, 0, 1) for dz in (-1, 1)}
        for dy in (-1, 0, 1):
            if blank_low is not None:
                deep[dy, -1] = jnp.where(blank_low, FAR, deep[dy, -1])
                deep[dy, 1] = jnp.where(blank_high, FAR, deep[dy, 1])
        for ey in (-1, 0, 1):
            if ey == 0:
                level = flat[0]
                ends = {dz: deep[0, dz] for dz in (-1, 1)}
            elif ey == 1:
                level = [
                    jnp.where(y == 3, turn(flat[1][k // 4], 48 - 16 * (k % 4)), turn(flat[0][k], -16))
                    for k in range(count)
                ]
                ends = {
                    dz: jnp.where(y == 3, turn(deep[1, dz], 48), turn(deep[0, dz], -16))
                    for dz in (-1, 1)
                }
            else:
                level = [
                    jnp.where(y == 0, turn(flat[-1][k // 4], -16 * (k % 4)), turn(flat[0][k], 16))
                    for k in range(count)
                ]
                ends = {
                    dz: jnp.where(y == 0, turn(deep[-1, dz], -48), turn(deep[0, dz], 16))
                    for dz in (-1, 1)
                }
            put((ex, ey, 0), level)
            put(
                (ex, ey, 1),
                [jnp.where(z == 15, turn(ends[1], 15 - k), turn(level[k], -1)) for k in range(count)],
            )
            put(
                (ex, ey, -1),
                [jnp.where(z == 0, turn(ends[-1], -k), turn(level[k], 1)) for k in range(count)],
            )


def kernel(
    position_arg, velocity_arg, kicks_arg, entry_arg, tally_arg, level_arg, fluence_arg,
    position_out, velocity_out, level_out,
    position_ref, velocity_ref, kicks_ref, entry_ref, tally_ref, level_in, fluence_ref,
    position_stage, velocity_stage, first_ref, rest_ref, heat_ref,
    first, rest, heat, position, velocity, shown, near, beside, beyond, near_slope, near_turned, density, force,
    affinity, pos_face, pos_land, slope_face, slope_land, level_ref, handed, choice,
    tile_out, tile_land, laser_out, laser_land, ext, ext_src,
    back_out, back_land, row_out, row_land,
    input_sem, first_sem, heat_sem, pos_sem, slope_sem, tile_sem, laser_sem, back_sem, row_sem,
):
    inputs = [
        pltpu.make_async_copy(
            arg, ref.at[pl.ds(0, arg.shape[0])] if len(arg.shape) == 2 and arg.shape[0] > 8 else ref,
            input_sem.at[k],
        )
        for k, (arg, ref) in enumerate(
            [
                (position_arg, position_ref), (tally_arg, tally_ref), (level_arg, level_in),
                (fluence_arg, fluence_ref), (velocity_arg, velocity_ref), (kicks_arg, kicks_ref),
                (entry_arg, entry_ref),
            ]
        )
    ]
    for copy in inputs:
        copy.start()
    gx, gy, gz = (lax.axis_index(a) for a in ("gx", "gy", "gz"))

    def x_place(tx):
        y = lax.rem(tx + 4, 8)
        return lax.rem(y, 4) * 2, y // 4

    def y_place(ty):
        return lax.rem(ty, 2), (ty // 2) * 2

    def device(xp, yp, tz):
        return (xp[0] + yp[0], xp[1] + yp[1], tz)

    tx = lax.rem(lax.rem(gy, 2) * 4 + gx // 2 + 4, 8)
    ty = (gy // 2) * 2 + lax.rem(gx, 2)
    tz = gz
    xs = {d: x_place(lax.rem(tx + d + 8, 8)) for d in range(-2, 3)}
    ys = {d: y_place(lax.rem(ty + d + 8, 8)) for d in (-1, 0, 1)}
    zs = {d: lax.rem(tz + d + 8, 8) for d in (-1, 0, 1)}

    def partner(d):
        return device(xs[d[0]], ys[d[1]], zs[d[2]])

    my_x, my_y = x_place(gx), y_place(gy)

    def worker(z):
        return device(my_x, my_y, z)

    def owner(z):
        return (tx, ty, z)

    barrier = pltpu.get_barrier_semaphore()
    greeted = [worker(z) for z in range(8)] + [owner(z) for z in range(8)]
    greeted += [partner(d) for d in (WIDE if REACH > 1 else AROUND)]
    for target in greeted:
        pl.semaphore_signal(barrier, inc=1, device_id=target, device_id_type=MESH)

    lane = lanes()
    row = lax.broadcasted_iota(jnp.int32, (8, 128), 0)
    slot = lax.broadcasted_iota(jnp.int32, (16, 128), 0)

    def by_lane(ref, base):
        return jnp.concatenate([ref[pl.ds(base + k, 16, stride=8), :] for k in range(8)], axis=1)

    inputs[0].wait()
    inputs[1].wait()
    for c in range(3):
        first_ref[16 * c : 16 * c + 16, :] = by_lane(position_ref, 128 * c)
    tally = jnp.concatenate([tally_ref[k // 4, k % 4 : k % 4 + 1, :] for k in range(8)], axis=1)
    first_ref[48:56, :] = jnp.broadcast_to(tally.astype(F32), (8, 128))
    pl.semaphore_wait(barrier, len(greeted))

    def send(src, dst, sems, target):
        pltpu.make_async_remote_copy(
            src_ref=src, dst_ref=dst, send_sem=sems.at[0], recv_sem=sems.at[1],
            device_id=target, device_id_type=MESH,
        ).start()

    def take(ref, sem):
        pltpu.make_async_copy(ref, ref, sem).wait()

    send(first_ref, first, first_sem.at[0], worker(gz))
    inputs[2].wait()
    inputs[3].wait()
    warm, fluence = jnp.zeros((8, 128), F32), jnp.zeros((8, 128), F32)
    for x in range(4):
        upper = jnp.broadcast_to(level_in[x, :, 0:128], (8, 128))
        lower = jnp.broadcast_to(level_in[x, :, 128:256], (8, 128))
        both = jnp.where(row < 4, upper, lower)
        for k in range(4):
            warm = jnp.where(((row & 3) == k) & ((lane >> 5) == x), turn(both, 32 * x - 32 * k), warm)
        fluence = jnp.where((lane >> 5) == x, fluence_ref[0:1, x : x + 1], fluence)
    heat_ref[:, 0, :] = warm
    heat_ref[:, 1, :] = fluence
    for z in range(8):
        send(heat_ref.at[z], heat.at[gz], heat_sem, worker(z))
    for copy in inputs[4:]:
        copy.wait()
    for c in range(3):
        rest_ref[16 * c : 16 * c + 16, :] = by_lane(velocity_ref, 128 * c)
    for c in range(6):
        rest_ref[48 + 16 * c : 64 + 16 * c, :] = by_lane(kicks_ref, 128 * c)
    rest_ref[144:160, :] = by_lane(entry_ref, 0).astype(F32)

    target = lax.broadcasted_iota(jnp.int32, (128, 128), 0)
    source = lax.broadcasted_iota(jnp.int32, (128, 128), 1)
    for k in range(4):
        wanted = (2 * (target >> 6) + k // 2) * 32 + 2 * (target & 15) + k % 2
        choice[128 * k : 128 * k + 128, :] = jnp.where(source == wanted, 1.0, 0.0).astype(F32)

    take(first, first_sem.at[0, 1])
    live = slot.astype(F32) < first[48:49, :]
    live3 = jnp.concatenate([live] * 3, axis=0)
    position[...] = first[0:48, :]
    at_bottom, at_top = tz == 0, tz == 7

    def spread(own, faces, face_ref, land, table, sems):
        at = 0
        places = {}
        for key, blocks in [(("x", 0), own)] + list(faces.items()):
            for k, block in enumerate(blocks):
                face_ref[at + 8 * k : at + 8 * k + 8, :] = block
            places[key] = (at, 8 * len(blocks))
            at += 8 * len(blocks)
        for d in AROUND:
            key = ("z", d[2]) if d[2] else ("y", d[1]) if d[1] else ("x", 0)
            start, rows = places[key]
            there = tuple(-c for c in d)
            send(
                face_ref.at[pl.ds(start, rows)], land.at[pl.ds(table[there][0], rows)],
                sems, partner(d),
            )

    tall = lax.broadcasted_iota(jnp.int32, (48, 128), 1)
    handed[...] = jnp.zeros((16, 128), F32)

    def dynamics(step, carry):
        own = pieces_of(jnp.where(live3, UNIT * position[...], FAR))
        for k, piece in enumerate(own):
            shown[8 * k : 8 * k + 8, :] = piece
        spread(own, packed(own), pos_face.at[step], pos_land.at[step], POS_ROWS, pos_sem.at[step])

        def put_position(e, pieces):
            index = CUBE.index(e)
            for k, piece in enumerate(pieces):
                near[index, 8 * k : 8 * k + 8, :] = piece + UNIT * e[k // 2]

        def sum_densities(there_ref, count, more):
            def two_densities(i, carry):
                homes = [[shown[pl.ds(16 * c + 2 * i + j, 1), :] for c in range(3)] for j in (0, 1)]
                totals = [jnp.zeros((16, 128), F32) for _ in (0, 1)]
                for index in range(count):
                    there = [there_ref[index, 16 * c : 16 * c + 16, :] for c in range(3)]
                    for j in (0, 1):
                        d = [there[c] - homes[j][c] for c in range(3)]
                        q = d[0] * d[0] + d[1] * d[1] + d[2] * d[2]
                        left = RANGE - q
                        w = jnp.maximum(left, 0.0)
                        totals[j] = totals[j] + jnp.exp2(left) * (w * w)
                for j in (0, 1):
                    at = pl.ds(2 * i + j, 1)
                    total = jnp.sum(totals[j], axis=0, keepdims=True)
                    density[at, :] = density[at, :] + total if more else total
                return carry

            lax.fori_loop(0, 8, two_densities, 0)

        empty = jnp.full((POS_TOTAL, 128), FAR, F32)
        neighbours(own, empty, POS_ROWS, None, None, put_position)
        sum_densities(near, 27, False)
        take(pos_land.at[step], pos_sem.at[step, 1])

        @pl.when(step == 0)
        def _():
            send(rest_ref, rest, first_sem.at[1], worker(gz))

        landed = pos_land[step]
        neighbours(own, landed, POS_ROWS, at_bottom, at_top, put_position)

        low_x, low_y, high_y = (tall >> 6) == 0, ((tall >> 4) & 3) == 0, ((tall >> 4) & 3) == 3
        low_z, high_z = (tall & 15) == 0, (tall & 15) == 15
        for a, ey in enumerate((-1, 0, 1)):
            for b, ez in enumerate((-1, 0, 1)):
                plus, minus = near[CUBE.index((1, ey, ez))], near[CUBE.index((-1, ey, ez))]
                beyond[3 * a + b] = jnp.where(low_x, minus, plus)
                beside[3 * a + b] = jnp.where(low_x, plus, minus)

        def within(half, ey, ez):
            return near[CUBE.index((0, ey, ez))] if half == 0 else beside[3 * ey + ez + 4]

        for half in (0, 1):
            for g in (-1, 0, 1):
                ends = jnp.where(
                    high_z, within(half, g, 1), jnp.where(low_z, within(half, g, -1), FAR)
                )
                beyond[9 + 5 * half + g + 1] = jnp.where(
                    high_y, within(half, 1, g), jnp.where(low_y, within(half, -1, g), ends)
                )
            level = jnp.where(
                high_z, within(half, 0, 1), jnp.where(low_z, within(half, 0, -1), FAR)
            )
            beyond[9 + 5 * half + 3] = jnp.where(low_y | high_y, level, FAR)
            inward = jnp.where(
                high_z, within(half, 1, 1), jnp.where(low_z, within(half, 1, -1), FAR)
            )
            outward = jnp.where(
                high_z, within(half, -1, 1), jnp.where(low_z, within(half, -1, -1), FAR)
            )
            beyond[9 + 5 * half + 4] = jnp.where(low_y, inward, jnp.where(high_y, outward, FAR))

        sum_densities(beyond, 19, True)
        rho = jnp.where(live, math.exp(-2.0) / RANGE**2 * density[...] - 1.0, 0.0)
        slope = -10.0 * lax.rsqrt(1.0 + jnp.maximum(rho, 0.0))
        density[...] = slope
        own_slope = pieces_of(slope)
        spread(
            own_slope, packed(own_slope), slope_face.at[step], slope_land.at[step], SLOPE_ROWS,
            slope_sem.at[step],
        )

        def two_geometries(i, carry):
            homes = [[shown[pl.ds(16 * c + 2 * i + j, 1), :] for c in range(3)] for j in (0, 1)]
            home_slopes = [density[pl.ds(2 * i + j, 1), :] for j in (0, 1)]
            totals = [[jnp.zeros((16, 128), F32) for _ in range(3)] for _ in (0, 1)]
            for index in range(27):
                there = [near[index, 16 * c : 16 * c + 16, :] for c in range(3)]
                for j in (0, 1):
                    d = [there[c] - homes[j][c] for c in range(3)]
                    q = d[0] * d[0] + d[1] * d[1] + d[2] * d[2]
                    w = jnp.maximum(RANGE - q, 0.0) * (1.0 / RANGE)
                    once = jnp.exp2(-0.5 * q)
                    common = w * (once * once)
                    embed = common * (w + 1.0)
                    affinity[2 * i + j, index] = embed
                    strength = embed * home_slopes[j] + common * once * (3.0 * w + 2.0)
                    totals[j] = [t + strength * c for t, c in zip(totals[j], d)]
            for j in (0, 1):
                for c in range(3):
                    force[pl.ds(16 * c + 2 * i + j, 1), :] = jnp.sum(
                        totals[j][c], axis=0, keepdims=True
                    )
            return carry

        lax.fori_loop(0, 8, two_geometries, 0)

        @pl.when(step == 0)
        def _():
            take(rest, first_sem.at[1, 1])
            take(heat, heat_sem.at[1])
            velocity[...] = rest[0:48, :]
            entry = rest[144:160, :]
            spread_out = lax.dot_general(
                heat[:, 0, :], choice[...], (((1,), (1,)), ((), ())),
                precision=lax.Precision.HIGHEST, preferred_element_type=F32,
            )
            level = jnp.zeros((16, 128), F32)
            for bx, bz, by in itertools.product((0, 1), repeat=3):
                k = 2 * bx + bz
                mine = row == 2 * ((lane >> 4) & 3) + by
                half = jnp.sum(
                    jnp.where(mine, spread_out[:, 128 * k : 128 * k + 128], 0.0), axis=0, keepdims=True
                )
                level = level + jnp.where(entry == float(4 * bx + 2 * by + bz), half, 0.0)
            level_ref[...] = jnp.sqrt(0.06 * level)
            laser_out[...] = heat[:, 1, :]
            for index, d in enumerate(FLAT):
                there = FLAT.index(tuple(-c for c in d))
                send(laser_out, laser_land.at[there], laser_sem, partner(d))

        take(slope_land.at[step], slope_sem.at[step, 1])

        def put_slope(e, pieces):
            index = CUBE.index(e)
            for k, piece in enumerate(pieces):
                near_slope[index, 8 * k : 8 * k + 8, :] = piece
                for c in range(3):
                    at = 16 * c + 8 * k
                    near_turned[index, at : at + 8, :] = piece * near[index, at : at + 8, :]

        neighbours(own_slope, slope_land[step], SLOPE_ROWS, None, None, put_slope)

        def two_forces(i, carry):
            plain = [jnp.zeros((16, 128), F32) for _ in (0, 1)]
            totals = [[jnp.zeros((16, 128), F32) for _ in range(3)] for _ in (0, 1)]
            for index in range(27):
                slopes = near_slope[index]
                turned = [near_turned[index, 16 * c : 16 * c + 16, :] for c in range(3)]
                for j in (0, 1):
                    embed = affinity[2 * i + j, index]
                    plain[j] = plain[j] + embed * slopes
                    totals[j] = [t + embed * c for t, c in zip(totals[j], turned)]
            for j in (0, 1):
                weight = jnp.sum(plain[j], axis=0, keepdims=True)
                for c in range(3):
                    at = pl.ds(16 * c + 2 * i + j, 1)
                    force[at, :] += jnp.sum(totals[j][c], axis=0, keepdims=True) - shown[at, :] * weight
            return carry

        lax.fori_loop(0, 8, two_forces, 0)

        old = velocity[...]
        kicks = rest[pl.ds(pl.multiple_of(48 + 48 * step, 16), 48), :]
        kicked = old + 0.03 * jnp.where(live3, (-2.0 / UNIT) * force[...], 0.0)
        noise = jnp.concatenate([level_ref[...]] * 3, axis=0)
        damped = 0.97 * kicked + noise * kicks
        gain = kicked * kicked - damped * damped
        handed[...] += jnp.where(live, 0.5 * (gain[0:16] + gain[16:32] + gain[32:48]), 0.0)
        velocity[...] = jnp.where(live3, damped, old)
        position[...] += 0.03 * jnp.where(live3, damped, 0.0)
        return carry

    lax.fori_loop(0, STEPS, dynamics, 0)

    back_out[0:48, :] = position[...]
    back_out[48:96, :] = velocity[...]

    entry = rest[144:160, :]
    placed = []
    for bx, bz in itertools.product((0, 1), repeat=2):
        low, high = (
            jnp.sum(
                jnp.where(entry == float(4 * bx + 2 * by + bz), handed[...], 0.0), axis=0, keepdims=True
            )
            for by in (0, 1)
        )
        rows_y = jnp.where((row & 1) == 1, high, low)
        placed.append(jnp.where((row >> 1) == ((lane >> 4) & 3), rows_y, 0.0))
    deposit = jnp.dot(
        jnp.concatenate(placed, axis=1), choice[...],
        precision=lax.Precision.HIGHEST, preferred_element_type=F32,
    )

    fold, place = lane >> 6, lane & 63
    depth = (lax.broadcasted_iota(jnp.int32, (24, 128), 1) & 63) + (32 * tz - 16)
    inner_face = (depth >= 0) & (depth < 255)

    def extend(tile_of, put):
        for i in range(FOLD):
            for yt in (-1, 0, 1):
                halves = []
                for h, x in ((0, i - HALO), (1, 3 + HALO - i)):
                    xt, xi = x // 4, x % 4
                    low, mid, high = (
                        turn(tile_of((xt, yt, zt)), 64 * h + 16 + 32 * zt - 32 * xi) for zt in (-1, 0, 1)
                    )
                    halves.append(jnp.where(place < 16, low, jnp.where(place < 48, mid, high)))
                put(i, 8 * yt + 8, jnp.where(fold == 0, halves[0], halves[1]))

    def conduct(t):
        square = 1.0 + t * t
        inverse = pl.reciprocal(square, approx=True)
        return 2.0 - inverse * (2.0 - square * inverse)

    def sweep(start):
        last = ext[start - 1]
        here = ext[start]
        k_here = conduct(here)
        before = (conduct(last) + k_here) * (here - last)
        for i in range(start, FOLD):
            if i < FOLD - 1:
                ahead = ext[i + 1]
                k_ahead = conduct(ahead)
            else:
                ahead, k_ahead = turn(here, 64), turn(k_here, 64)
            after = (k_here + k_ahead) * (ahead - here)
            up_y = (k_here + turn(k_here, -1, 0)) * (turn(here, -1, 0) - here)
            up_z = (k_here + turn(k_here, -1)) * (turn(here, -1) - here)
            up_z = jnp.where(inner_face, up_z, 0.0)
            net = (after - before) + (up_y - turn(up_y, 1, 0)) + (up_z - turn(up_z, 1))
            ext[i] = here + 0.04 * net + ext_src[i]
            before, here, k_here = after, ahead, k_ahead

    def centre():
        tile = None
        for x in range(4):
            h = x // 2
            moved = turn(ext[HALO + (x if h == 0 else 3 - x), 8:16, :], 32 * x - 64 * h - 16)
            tile = moved if tile is None else jnp.where((lane >> 5) == x, moved, tile)
        return tile

    def put_level(i, at, block):
        ext[i, at : at + 8, :] = block

    decay = (lane & 63).astype(F32) + ((32 * tz).astype(F32) - 15.5)
    decay = 0.02 * jnp.exp(decay * (-1.0 / 64.0))

    def put_source(i, at, block):
        ext_src[i, at : at + 8, :] = block * decay

    for turn_of in range(ROUNDS):
        out, land = tile_out.at[turn_of], tile_land.at[turn_of]
        if turn_of == 0:
            out[...] = heat[:, 0, :] + 0.5 * deposit
        else:
            out[...] = centre()
        for index, d in enumerate(WIDE):
            there = WIDE.index(tuple(-c for c in d))
            send(out, land.at[there], tile_sem.at[turn_of], partner(d))
        if turn_of == 0:
            send(back_out, back_land, back_sem, owner(tz))
            take(laser_land, laser_sem.at[1])

            def laser_of(d):
                d = (d[0], d[1], 0)
                return laser_out[...] if d == (0, 0, 0) else laser_land[FLAT.index(d)]

            extend(laser_of, put_source)
        if turn_of == ROUNDS - 1:
            take(back_land, back_sem.at[1])
            for ref, at in ((position_stage, 0), (velocity_stage, 48)):
                for c in range(3):
                    block = back_land[at + 16 * c : at + 16 * c + 16, :]
                    for k in range(8):
                        ref[pl.ds(128 * c + k, 16, stride=8), :] = block[:, 16 * k : 16 * k + 16]
        if turn_of == ROUNDS - 1:
            position_out[...] = position_stage[0:384, :]
            velocity_out[...] = velocity_stage[0:384, :]
        take(land, tile_sem.at[turn_of, 1])
        extend(lambda d: out[...] if d == (0, 0, 0) else land[WIDE.index(d)], put_level)
        for start in range(1, HALO + 1):
            sweep(start)

    result = centre()
    for y in range(8):
        row_out[y, :, :] = result[y : y + 1]
        send(row_out.at[y], row_land.at[tz], row_sem, owner(y))

    take(first_ref, first_sem.at[0, 0])
    take(rest_ref, first_sem.at[1, 0])
    take(heat_ref, heat_sem.at[0])
    for step in range(STEPS):
        take(pos_land.at[step], pos_sem.at[step, 0])
        take(slope_land.at[step], slope_sem.at[step, 0])
    take(laser_land, laser_sem.at[0])
    for turn_of in range(ROUNDS):
        take(tile_land.at[turn_of], tile_sem.at[turn_of, 0])
    take(back_out, back_sem.at[0])
    take(row_out, row_sem.at[0])

    take(row_land, row_sem.at[1])
    rows = row_land[:, 0, :]
    for x in range(4):
        line = jnp.zeros((8, 128), F32)
        for k in range(4):
            line = jnp.where(
                ((row & 3) == k) & ((lane >> 5) == k), turn(rows, 32 * k - 32 * x), line
            )
        level_out[x, :, 0:128] = jnp.sum(line[0:4], axis=0, keepdims=True)
        level_out[x, :, 128:256] = jnp.sum(line[4:8], axis=0, keepdims=True)


def deliver(*refs):
    sources, results, stops, sem = refs[:3], refs[3:6], refs[6:9], refs[9]
    copies = [
        [pltpu.make_async_copy(src, dst, sem.at[leg, k]) for k, (src, dst) in enumerate(pairs)]
        for leg, pairs in enumerate((zip(sources, stops), zip(stops, results)))
    ]
    for copy in copies[0]:
        copy.start()
    for copy, onward in zip(*copies):
        copy.wait()
        onward.start()
    for copy in copies[1]:
        copy.wait()


def face_rows(pieces):
    return 8 * (pieces + 2 + 2 * ((pieces + 3) // 4))


def shards(
    particle_local_offsets,
    particle_velocity,
    stochastic_kicks,
    thermal_mesh_entry,
    occupant_tally,
    fermion_thermal_level,
    fluence_profile,
):
    vmem = pl.BlockSpec(memory_space=pltpu.VMEM)
    args = (
        particle_local_offsets.reshape(384, 16),
        particle_velocity.reshape(384, 16),
        stochastic_kicks.reshape(768, 16),
        thermal_mesh_entry.reshape(128, 16),
        occupant_tally,
        fermion_thermal_level,
        fluence_profile.T,
    )
    buffers = [
        (56, 128), (160, 128), (8, 2, 128),
        (56, 128), (160, 128), (8, 2, 128), (48, 128), (48, 128), (48, 128),
        (27, 48, 128), (9, 48, 128), (19, 48, 128), (27, 16, 128), (27, 48, 128), (16, 128), (48, 128),
        (16, 27, 16, 128), (STEPS, face_rows(6), 128), (STEPS, POS_TOTAL, 128),
        (STEPS, face_rows(2), 128), (STEPS, SLOPE_TOTAL, 128), (16, 128), (16, 128), (512, 128),
        (ROUNDS, 8, 128), (ROUNDS, len(WIDE), 8, 128), (8, 128), (len(FLAT), 8, 128),
        (FOLD, 24, 128), (FOLD, 24, 128),
        (96, 128), (96, 128), (8, 1, 128), (8, 1, 128),
    ]
    sems = [(7,), (2, 2), (2,), (STEPS, 2), (STEPS, 2), (ROUNDS, 2), (2,), (2,), (2,)]
    position, velocity, level = pl.pallas_call(
        kernel,
        out_shape=(
            jax.ShapeDtypeStruct((384, 16), F32),
            jax.ShapeDtypeStruct((384, 16), F32),
            jax.ShapeDtypeStruct(fermion_thermal_level.shape, F32),
        ),
        in_specs=[pl.BlockSpec(memory_space=pltpu.HBM)] * 7,
        out_specs=(vmem, vmem, vmem),
        scratch_shapes=[pltpu.VMEM((arg.shape[0] + 8, 16), arg.dtype) for arg in args[:4]]
        + [pltpu.VMEM(arg.shape, arg.dtype) for arg in args[4:]]
        + [pltpu.VMEM((392, 16), F32)] * 2
        + [pltpu.VMEM(shape, F32) for shape in buffers]
        + [pltpu.SemaphoreType.DMA(shape) for shape in sems],
        compiler_params=pltpu.CompilerParams(
            collective_id=0, has_side_effects=True, vmem_limit_bytes=60 * 1024 * 1024
        ),
    )(*args)
    results = (position, velocity, level)
    position, velocity, level = pl.pallas_call(
        deliver,
        out_shape=tuple(jax.ShapeDtypeStruct(result.shape, F32) for result in results),
        in_specs=[pl.BlockSpec(memory_space=pltpu.HBM)] * 3,
        out_specs=(pl.BlockSpec(memory_space=pltpu.HBM),) * 3,
        scratch_shapes=[pltpu.VMEM(result.shape, F32) for result in results]
        + [pltpu.SemaphoreType.DMA((2, 3))],
        compiler_params=pltpu.CompilerParams(vmem_limit_bytes=60 * 1024 * 1024),
    )(*results)
    shape = particle_local_offsets.shape
    return position.reshape(shape), velocity.reshape(shape), level


def solution(mesh):
    placed = (
        P(None, None, "gx", "gy", "gz"),
        P(None, None, "gx", "gy", "gz"),
        P(None, None, None, "gx", "gy", "gz"),
        P(None, "gx", "gy", "gz"),
        P("gx", "gy", "gz"),
        P("gx", ("gy", "gz"), None),
        P("gx", ("gy", "gz")),
    )
    return jax.shard_map(
        shards,
        mesh=mesh,
        in_specs=placed,
        out_specs=(
            P(None, None, "gx", "gy", "gz"),
            P(None, None, "gx", "gy", "gz"),
            P("gx", ("gy", "gz"), None),
        ),
        check_vma=False,
    )
```

```python
import itertools
import math

import jax
import jax.numpy as jnp
from jax import lax
from jax.experimental import pallas as pl
from jax.experimental.pallas import tpu as pltpu
from jax.sharding import PartitionSpec as P

MESH = pl.DeviceIdType.MESH
F32 = jnp.float32
STEPS = 2
HALO = 8
ROUNDS = 16 // HALO
REACH = HALO // 4
RANGE = 2.0 * math.log2(math.e)
UNIT = math.sqrt(RANGE)
FAR = 1.0e6
CUBE = [d for d in itertools.product((-1, 0, 1), repeat=3)]
AROUND = sorted((d for d in CUBE if d != (0, 0, 0)), key=lambda d: -sum(map(abs, d)))
WIDE = sorted(
    (
        d
        for d in itertools.product(range(-REACH, REACH + 1), (-1, 0, 1), (-1, 0, 1))
        if d != (0, 0, 0)
    ),
    key=lambda d: -sum(map(abs, d)),
)
FOLD = (4 + 2 * HALO) // 2
FLAT = [d for d in WIDE if d[2] == 0]


def parts_of(pieces):
    rows, start = {}, 0
    for d in AROUND:
        if d[2] != 0:
            count = 8
        elif d[1] != 0:
            count = 8 * ((pieces + 3) // 4)
        else:
            count = 8 * pieces
        rows[d] = (start, count)
        start += count
    return rows, start


POS_ROWS, POS_TOTAL = parts_of(6)
SLOPE_ROWS, SLOPE_TOTAL = parts_of(2)


def turn(block, shift, axis=1):
    size = block.shape[axis]
    shift = shift % size
    return block if shift == 0 else pltpu.roll(block, shift, axis)


def lanes(rows=8):
    return lax.broadcasted_iota(jnp.int32, (rows, 128), 1)


def pieces_of(block):
    return [block[8 * k : 8 * k + 8] for k in range(block.shape[0] // 8)]


def packed(pieces):
    lane = lanes()
    y, z = (lane >> 4) & 3, lane & 15
    faces = {}
    for dz in (1, -1):
        face = pieces[0]
        for k, piece in enumerate(pieces):
            moved = turn(piece, k - 15 if dz == 1 else k)
            face = moved if k == 0 else jnp.where(z == k, moved, face)
        faces["z", dz] = [face]
    for dy in (1, -1):
        blocks = []
        for first in range(0, len(pieces), 4):
            face = None
            for k, piece in enumerate(pieces[first : first + 4]):
                moved = turn(piece, 16 * k - 48 if dy == 1 else 16 * k)
                face = moved if face is None else jnp.where(y == k, moved, face)
            blocks.append(face)
        faces["y", dy] = blocks
    return faces


def face_start(table, d):
    return table[d][0], table[d][1]


def neighbours(own, landed, table, blank_low, blank_high, put):
    lane = lanes()
    x, y, z = lane >> 6, (lane >> 4) & 3, lane & 15
    count = len(own)

    def column(dx, dy, dz):
        if (dx, dy, dz) == (0, 0, 0):
            return own
        start, rows = table[dx, dy, dz]
        return pieces_of(landed[start : start + rows])

    for ex in (-1, 0, 1):

        def along_x(dy, dz):
            here = column(0, dy, dz)
            if ex == 0:
                return here
            there = column(ex, dy, dz)
            if ex == 1:
                return [turn(jnp.where(x == 0, b, a), 64) for a, b in zip(here, there)]
            return [turn(jnp.where(x == 0, a, b), 64) for a, b in zip(here, there)]

        flat = {dy: along_x(dy, 0) for dy in (-1, 0, 1)}
        deep = {(dy, dz): along_x(dy, dz)[0] for dy in (-1, 0, 1) for dz in (-1, 1)}
        for dy in (-1, 0, 1):
            if blank_low is not None:
                deep[dy, -1] = jnp.where(blank_low, FAR, deep[dy, -1])
                deep[dy, 1] = jnp.where(blank_high, FAR, deep[dy, 1])
        for ey in (-1, 0, 1):
            if ey == 0:
                level = flat[0]
                ends = {dz: deep[0, dz] for dz in (-1, 1)}
            elif ey == 1:
                level = [
                    jnp.where(y == 3, turn(flat[1][k // 4], 48 - 16 * (k % 4)), turn(flat[0][k], -16))
                    for k in range(count)
                ]
                ends = {
                    dz: jnp.where(y == 3, turn(deep[1, dz], 48), turn(deep[0, dz], -16))
                    for dz in (-1, 1)
                }
            else:
                level = [
                    jnp.where(y == 0, turn(flat[-1][k // 4], -16 * (k % 4)), turn(flat[0][k], 16))
                    for k in range(count)
                ]
                ends = {
                    dz: jnp.where(y == 0, turn(deep[-1, dz], -48), turn(deep[0, dz], 16))
                    for dz in (-1, 1)
                }
            put((ex, ey, 0), level)
            put(
                (ex, ey, 1),
                [jnp.where(z == 15, turn(ends[1], 15 - k), turn(level[k], -1)) for k in range(count)],
            )
            put(
                (ex, ey, -1),
                [jnp.where(z == 0, turn(ends[-1], -k), turn(level[k], 1)) for k in range(count)],
            )


def kernel(
    position_arg, velocity_arg, kicks_arg, entry_arg, tally_arg, level_arg, fluence_arg,
    position_out, velocity_out, level_out,
    position_ref, velocity_ref, kicks_ref, entry_ref, tally_ref, level_in, fluence_ref,
    position_stage, velocity_stage, first_ref, rest_ref, heat_ref,
    first, rest, heat, position, velocity, shown, near, beside, beyond, near_slope, near_turned, density, force,
    affinity, pos_face, pos_land, slope_face, slope_land, level_ref, handed, choice,
    tile_out, tile_land, laser_out, laser_land, ext, ext_src,
    back_out, back_land, row_out, row_land,
    input_sem, first_sem, heat_sem, pos_sem, slope_sem, tile_sem, laser_sem, back_sem, row_sem, leave_sem,
):
    inputs = [
        pltpu.make_async_copy(
            arg, ref.at[pl.ds(0, arg.shape[0])] if len(arg.shape) == 2 and arg.shape[0] > 8 else ref,
            input_sem.at[k],
        )
        for k, (arg, ref) in enumerate(
            [
                (position_arg, position_ref), (tally_arg, tally_ref), (level_arg, level_in),
                (fluence_arg, fluence_ref), (velocity_arg, velocity_ref), (kicks_arg, kicks_ref),
                (entry_arg, entry_ref),
            ]
        )
    ]
    for copy in inputs:
        copy.start()
    gx, gy, gz = (lax.axis_index(a) for a in ("gx", "gy", "gz"))

    def x_place(tx):
        y = lax.rem(tx + 4, 8)
        return lax.rem(y, 4) * 2, y // 4

    def y_place(ty):
        return lax.rem(ty, 2), (ty // 2) * 2

    def device(xp, yp, tz):
        return (xp[0] + yp[0], xp[1] + yp[1], tz)

    tx = lax.rem(lax.rem(gy, 2) * 4 + gx // 2 + 4, 8)
    ty = (gy // 2) * 2 + lax.rem(gx, 2)
    tz = gz
    xs = {d: x_place(lax.rem(tx + d + 8, 8)) for d in range(-2, 3)}
    ys = {d: y_place(lax.rem(ty + d + 8, 8)) for d in (-1, 0, 1)}
    zs = {d: lax.rem(tz + d + 8, 8) for d in (-1, 0, 1)}

    def partner(d):
        return device(xs[d[0]], ys[d[1]], zs[d[2]])

    my_x, my_y = x_place(gx), y_place(gy)

    def worker(z):
        return device(my_x, my_y, z)

    def owner(z):
        return (tx, ty, z)

    barrier = pltpu.get_barrier_semaphore()
    greeted = [worker(z) for z in range(8)] + [owner(z) for z in range(8)]
    greeted += [partner(d) for d in (WIDE if REACH > 1 else AROUND)]
    for target in greeted:
        pl.semaphore_signal(barrier, inc=1, device_id=target, device_id_type=MESH)

    lane = lanes()
    row = lax.broadcasted_iota(jnp.int32, (8, 128), 0)
    slot = lax.broadcasted_iota(jnp.int32, (16, 128), 0)

    def by_lane(ref, base):
        return jnp.concatenate([ref[pl.ds(base + k, 16, stride=8), :] for k in range(8)], axis=1)

    inputs[0].wait()
    inputs[1].wait()
    for c in range(3):
        first_ref[16 * c : 16 * c + 16, :] = by_lane(position_ref, 128 * c)
    tally = jnp.concatenate([tally_ref[k // 4, k % 4 : k % 4 + 1, :] for k in range(8)], axis=1)
    first_ref[48:56, :] = jnp.broadcast_to(tally.astype(F32), (8, 128))
    pl.semaphore_wait(barrier, len(greeted))

    def send(src, dst, sems, target):
        pltpu.make_async_remote_copy(
            src_ref=src, dst_ref=dst, send_sem=sems.at[0], recv_sem=sems.at[1],
            device_id=target, device_id_type=MESH,
        ).start()

    def take(ref, sem):
        pltpu.make_async_copy(ref, ref, sem).wait()

    send(first_ref, first, first_sem.at[0], worker(gz))
    inputs[2].wait()
    inputs[3].wait()
    warm, fluence = jnp.zeros((8, 128), F32), jnp.zeros((8, 128), F32)
    for x in range(4):
        upper = jnp.broadcast_to(level_in[x, :, 0:128], (8, 128))
        lower = jnp.broadcast_to(level_in[x, :, 128:256], (8, 128))
        both = jnp.where(row < 4, upper, lower)
        for k in range(4):
            warm = jnp.where(((row & 3) == k) & ((lane >> 5) == x), turn(both, 32 * x - 32 * k), warm)
        fluence = jnp.where((lane >> 5) == x, fluence_ref[0:1, x : x + 1], fluence)
    heat_ref[:, 0, :] = warm
    heat_ref[:, 1, :] = fluence
    for z in range(8):
        send(heat_ref.at[z], heat.at[gz], heat_sem, worker(z))
    for copy in inputs[4:]:
        copy.wait()
    for c in range(3):
        rest_ref[16 * c : 16 * c + 16, :] = by_lane(velocity_ref, 128 * c)
    for c in range(6):
        rest_ref[48 + 16 * c : 64 + 16 * c, :] = by_lane(kicks_ref, 128 * c)
    rest_ref[144:160, :] = by_lane(entry_ref, 0).astype(F32)

    target = lax.broadcasted_iota(jnp.int32, (128, 128), 0)
    source = lax.broadcasted_iota(jnp.int32, (128, 128), 1)
    for k in range(4):
        wanted = (2 * (target >> 6) + k // 2) * 32 + 2 * (target & 15) + k % 2
        choice[128 * k : 128 * k + 128, :] = jnp.where(source == wanted, 1.0, 0.0).astype(F32)

    take(first, first_sem.at[0, 1])
    live = slot.astype(F32) < first[48:49, :]
    live3 = jnp.concatenate([live] * 3, axis=0)
    position[...] = first[0:48, :]
    at_bottom, at_top = tz == 0, tz == 7

    def spread(own, faces, face_ref, land, table, sems):
        at = 0
        places = {}
        for key, blocks in [(("x", 0), own)] + list(faces.items()):
            for k, block in enumerate(blocks):
                face_ref[at + 8 * k : at + 8 * k + 8, :] = block
            places[key] = (at, 8 * len(blocks))
            at += 8 * len(blocks)
        for d in AROUND:
            key = ("z", d[2]) if d[2] else ("y", d[1]) if d[1] else ("x", 0)
            start, rows = places[key]
            there = tuple(-c for c in d)
            send(
                face_ref.at[pl.ds(start, rows)], land.at[pl.ds(table[there][0], rows)],
                sems, partner(d),
            )

    tall = lax.broadcasted_iota(jnp.int32, (48, 128), 1)
    handed[...] = jnp.zeros((16, 128), F32)

    def dynamics(step, carry):
        own = pieces_of(jnp.where(live3, UNIT * position[...], FAR))
        for k, piece in enumerate(own):
            shown[8 * k : 8 * k + 8, :] = piece
        spread(own, packed(own), pos_face.at[step], pos_land.at[step], POS_ROWS, pos_sem.at[step])

        def put_position(e, pieces):
            index = CUBE.index(e)
            for k, piece in enumerate(pieces):
                near[index, 8 * k : 8 * k + 8, :] = piece + UNIT * e[k // 2]

        def sum_densities(there_ref, count, more):
            def two_densities(i, carry):
                homes = [[shown[pl.ds(16 * c + 2 * i + j, 1), :] for c in range(3)] for j in (0, 1)]
                totals = [jnp.zeros((16, 128), F32) for _ in (0, 1)]
                for index in range(count):
                    there = [there_ref[index, 16 * c : 16 * c + 16, :] for c in range(3)]
                    for j in (0, 1):
                        d = [there[c] - homes[j][c] for c in range(3)]
                        q = d[0] * d[0] + d[1] * d[1] + d[2] * d[2]
                        left = RANGE - q
                        w = jnp.maximum(left, 0.0)
                        totals[j] = totals[j] + jnp.exp2(left) * (w * w)
                for j in (0, 1):
                    at = pl.ds(2 * i + j, 1)
                    total = jnp.sum(totals[j], axis=0, keepdims=True)
                    density[at, :] = density[at, :] + total if more else total
                return carry

            lax.fori_loop(0, 8, two_densities, 0)

        empty = jnp.full((POS_TOTAL, 128), FAR, F32)
        neighbours(own, empty, POS_ROWS, None, None, put_position)
        sum_densities(near, 27, False)
        take(pos_land.at[step], pos_sem.at[step, 1])

        @pl.when(step == 0)
        def _():
            send(rest_ref, rest, first_sem.at[1], worker(gz))

        landed = pos_land[step]
        neighbours(own, landed, POS_ROWS, at_bottom, at_top, put_position)

        low_x, low_y, high_y = (tall >> 6) == 0, ((tall >> 4) & 3) == 0, ((tall >> 4) & 3) == 3
        low_z, high_z = (tall & 15) == 0, (tall & 15) == 15
        for a, ey in enumerate((-1, 0, 1)):
            for b, ez in enumerate((-1, 0, 1)):
                plus, minus = near[CUBE.index((1, ey, ez))], near[CUBE.index((-1, ey, ez))]
                beyond[3 * a + b] = jnp.where(low_x, minus, plus)
                beside[3 * a + b] = jnp.where(low_x, plus, minus)

        def within(half, ey, ez):
            return near[CUBE.index((0, ey, ez))] if half == 0 else beside[3 * ey + ez + 4]

        for half in (0, 1):
            for g in (-1, 0, 1):
                ends = jnp.where(
                    high_z, within(half, g, 1), jnp.where(low_z, within(half, g, -1), FAR)
                )
                beyond[9 + 5 * half + g + 1] = jnp.where(
                    high_y, within(half, 1, g), jnp.where(low_y, within(half, -1, g), ends)
                )
            level = jnp.where(
                high_z, within(half, 0, 1), jnp.where(low_z, within(half, 0, -1), FAR)
            )
            beyond[9 + 5 * half + 3] = jnp.where(low_y | high_y, level, FAR)
            inward = jnp.where(
                high_z, within(half, 1, 1), jnp.where(low_z, within(half, 1, -1), FAR)
            )
            outward = jnp.where(
                high_z, within(half, -1, 1), jnp.where(low_z, within(half, -1, -1), FAR)
            )
            beyond[9 + 5 * half + 4] = jnp.where(low_y, inward, jnp.where(high_y, outward, FAR))

        sum_densities(beyond, 19, True)
        rho = jnp.where(live, math.exp(-2.0) / RANGE**2 * density[...] - 1.0, 0.0)
        slope = -10.0 * lax.rsqrt(1.0 + jnp.maximum(rho, 0.0))
        density[...] = slope
        own_slope = pieces_of(slope)
        spread(
            own_slope, packed(own_slope), slope_face.at[step], slope_land.at[step], SLOPE_ROWS,
            slope_sem.at[step],
        )

        def two_geometries(i, carry):
            homes = [[shown[pl.ds(16 * c + 2 * i + j, 1), :] for c in range(3)] for j in (0, 1)]
            home_slopes = [density[pl.ds(2 * i + j, 1), :] for j in (0, 1)]
            totals = [[jnp.zeros((16, 128), F32) for _ in range(3)] for _ in (0, 1)]
            for index in range(27):
                there = [near[index, 16 * c : 16 * c + 16, :] for c in range(3)]
                for j in (0, 1):
                    d = [there[c] - homes[j][c] for c in range(3)]
                    q = d[0] * d[0] + d[1] * d[1] + d[2] * d[2]
                    w = jnp.maximum(RANGE - q, 0.0) * (1.0 / RANGE)
                    once = jnp.exp2(-0.5 * q)
                    common = w * (once * once)
                    embed = common * (w + 1.0)
                    affinity[2 * i + j, index] = embed
                    strength = embed * home_slopes[j] + common * once * (3.0 * w + 2.0)
                    totals[j] = [t + strength * c for t, c in zip(totals[j], d)]
            for j in (0, 1):
                for c in range(3):
                    force[pl.ds(16 * c + 2 * i + j, 1), :] = jnp.sum(
                        totals[j][c], axis=0, keepdims=True
                    )
            return carry

        lax.fori_loop(0, 8, two_geometries, 0)

        @pl.when(step == 0)
        def _():
            take(rest, first_sem.at[1, 1])
            take(heat, heat_sem.at[1])
            velocity[...] = rest[0:48, :]
            entry = rest[144:160, :]
            spread_out = lax.dot_general(
                heat[:, 0, :], choice[...], (((1,), (1,)), ((), ())),
                precision=lax.Precision.HIGHEST, preferred_element_type=F32,
            )
            level = jnp.zeros((16, 128), F32)
            for bx, bz, by in itertools.product((0, 1), repeat=3):
                k = 2 * bx + bz
                mine = row == 2 * ((lane >> 4) & 3) + by
                half = jnp.sum(
                    jnp.where(mine, spread_out[:, 128 * k : 128 * k + 128], 0.0), axis=0, keepdims=True
                )
                level = level + jnp.where(entry == float(4 * bx + 2 * by + bz), half, 0.0)
            level_ref[...] = jnp.sqrt(0.06 * level)
            laser_out[...] = heat[:, 1, :]
            for index, d in enumerate(FLAT):
                there = FLAT.index(tuple(-c for c in d))
                send(laser_out, laser_land.at[there], laser_sem, partner(d))

        take(slope_land.at[step], slope_sem.at[step, 1])

        def put_slope(e, pieces):
            index = CUBE.index(e)
            for k, piece in enumerate(pieces):
                near_slope[index, 8 * k : 8 * k + 8, :] = piece
                for c in range(3):
                    at = 16 * c + 8 * k
                    near_turned[index, at : at + 8, :] = piece * near[index, at : at + 8, :]

        neighbours(own_slope, slope_land[step], SLOPE_ROWS, None, None, put_slope)

        def two_forces(i, carry):
            plain = [jnp.zeros((16, 128), F32) for _ in (0, 1)]
            totals = [[jnp.zeros((16, 128), F32) for _ in range(3)] for _ in (0, 1)]
            for index in range(27):
                slopes = near_slope[index]
                turned = [near_turned[index, 16 * c : 16 * c + 16, :] for c in range(3)]
                for j in (0, 1):
                    embed = affinity[2 * i + j, index]
                    plain[j] = plain[j] + embed * slopes
                    totals[j] = [t + embed * c for t, c in zip(totals[j], turned)]
            for j in (0, 1):
                weight = jnp.sum(plain[j], axis=0, keepdims=True)
                for c in range(3):
                    at = pl.ds(16 * c + 2 * i + j, 1)
                    force[at, :] += jnp.sum(totals[j][c], axis=0, keepdims=True) - shown[at, :] * weight
            return carry

        lax.fori_loop(0, 8, two_forces, 0)

        old = velocity[...]
        kicks = rest[pl.ds(pl.multiple_of(48 + 48 * step, 16), 48), :]
        kicked = old + 0.03 * jnp.where(live3, (-2.0 / UNIT) * force[...], 0.0)
        noise = jnp.concatenate([level_ref[...]] * 3, axis=0)
        damped = 0.97 * kicked + noise * kicks
        gain = kicked * kicked - damped * damped
        handed[...] += jnp.where(live, 0.5 * (gain[0:16] + gain[16:32] + gain[32:48]), 0.0)
        velocity[...] = jnp.where(live3, damped, old)
        position[...] += 0.03 * jnp.where(live3, damped, 0.0)
        return carry

    lax.fori_loop(0, STEPS, dynamics, 0)

    back_out[0:48, :] = position[...]
    back_out[48:96, :] = velocity[...]

    entry = rest[144:160, :]
    placed = []
    for bx, bz in itertools.product((0, 1), repeat=2):
        low, high = (
            jnp.sum(
                jnp.where(entry == float(4 * bx + 2 * by + bz), handed[...], 0.0), axis=0, keepdims=True
            )
            for by in (0, 1)
        )
        rows_y = jnp.where((row & 1) == 1, high, low)
        placed.append(jnp.where((row >> 1) == ((lane >> 4) & 3), rows_y, 0.0))
    deposit = jnp.dot(
        jnp.concatenate(placed, axis=1), choice[...],
        precision=lax.Precision.HIGHEST, preferred_element_type=F32,
    )

    fold, place = lane >> 6, lane & 63
    depth = (lax.broadcasted_iota(jnp.int32, (24, 128), 1) & 63) + (32 * tz - 16)
    inner_face = (depth >= 0) & (depth < 255)

    def extend(tile_of, put):
        for i in range(FOLD):
            for yt in (-1, 0, 1):
                halves = []
                for h, x in ((0, i - HALO), (1, 3 + HALO - i)):
                    xt, xi = x // 4, x % 4
                    low, mid, high = (
                        turn(tile_of((xt, yt, zt)), 64 * h + 16 + 32 * zt - 32 * xi) for zt in (-1, 0, 1)
                    )
                    halves.append(jnp.where(place < 16, low, jnp.where(place < 48, mid, high)))
                put(i, 8 * yt + 8, jnp.where(fold == 0, halves[0], halves[1]))

    def conduct(t):
        square = 1.0 + t * t
        inverse = pl.reciprocal(square, approx=True)
        return 2.0 - inverse * (2.0 - square * inverse)

    def sweep(start):
        last = ext[start - 1]
        here = ext[start]
        k_here = conduct(here)
        before = (conduct(last) + k_here) * (here - last)
        for i in range(start, FOLD):
            if i < FOLD - 1:
                ahead = ext[i + 1]
                k_ahead = conduct(ahead)
            else:
                ahead, k_ahead = turn(here, 64), turn(k_here, 64)
            after = (k_here + k_ahead) * (ahead - here)
            up_y = (k_here + turn(k_here, -1, 0)) * (turn(here, -1, 0) - here)
            up_z = (k_here + turn(k_here, -1)) * (turn(here, -1) - here)
            up_z = jnp.where(inner_face, up_z, 0.0)
            net = (after - before) + (up_y - turn(up_y, 1, 0)) + (up_z - turn(up_z, 1))
            ext[i] = here + 0.04 * net + ext_src[i]
            before, here, k_here = after, ahead, k_ahead

    def centre():
        tile = None
        for x in range(4):
            h = x // 2
            moved = turn(ext[HALO + (x if h == 0 else 3 - x), 8:16, :], 32 * x - 64 * h - 16)
            tile = moved if tile is None else jnp.where((lane >> 5) == x, moved, tile)
        return tile

    def put_level(i, at, block):
        ext[i, at : at + 8, :] = block

    decay = (lane & 63).astype(F32) + ((32 * tz).astype(F32) - 15.5)
    decay = 0.02 * jnp.exp(decay * (-1.0 / 64.0))

    def put_source(i, at, block):
        ext_src[i, at : at + 8, :] = block * decay

    leaving = [
        pltpu.make_async_copy(stage.at[pl.ds(0, 384)], ref, leave_sem.at[k])
        for k, (stage, ref) in enumerate(
            [(position_stage, position_out), (velocity_stage, velocity_out)]
        )
    ]
    for turn_of in range(ROUNDS):
        out, land = tile_out.at[turn_of], tile_land.at[turn_of]
        if turn_of == 0:
            out[...] = heat[:, 0, :] + 0.5 * deposit
        else:
            out[...] = centre()
        for index, d in enumerate(WIDE):
            there = WIDE.index(tuple(-c for c in d))
            send(out, land.at[there], tile_sem.at[turn_of], partner(d))
        if turn_of == 0:
            send(back_out, back_land, back_sem, owner(tz))
            take(laser_land, laser_sem.at[1])

            def laser_of(d):
                d = (d[0], d[1], 0)
                return laser_out[...] if d == (0, 0, 0) else laser_land[FLAT.index(d)]

            extend(laser_of, put_source)
        if turn_of == ROUNDS - 1:
            take(back_land, back_sem.at[1])
            for ref, at in ((position_stage, 0), (velocity_stage, 48)):
                for c in range(3):
                    block = back_land[at + 16 * c : at + 16 * c + 16, :]
                    for k in range(8):
                        ref[pl.ds(128 * c + k, 16, stride=8), :] = block[:, 16 * k : 16 * k + 16]
        if turn_of == ROUNDS - 1:
            for copy in leaving:
                copy.start()
        take(land, tile_sem.at[turn_of, 1])
        extend(lambda d: out[...] if d == (0, 0, 0) else land[WIDE.index(d)], put_level)
        for start in range(1, HALO + 1):
            sweep(start)

    result = centre()
    for y in range(8):
        row_out[y, :, :] = result[y : y + 1]
        send(row_out.at[y], row_land.at[tz], row_sem, owner(y))

    take(first_ref, first_sem.at[0, 0])
    take(rest_ref, first_sem.at[1, 0])
    take(heat_ref, heat_sem.at[0])
    for step in range(STEPS):
        take(pos_land.at[step], pos_sem.at[step, 0])
        take(slope_land.at[step], slope_sem.at[step, 0])
    take(laser_land, laser_sem.at[0])
    for turn_of in range(ROUNDS):
        take(tile_land.at[turn_of], tile_sem.at[turn_of, 0])
    take(back_out, back_sem.at[0])
    take(row_out, row_sem.at[0])

    for copy in leaving:
        copy.wait()
    take(row_land, row_sem.at[1])
    rows = row_land[:, 0, :]
    for x in range(4):
        line = jnp.zeros((8, 128), F32)
        for k in range(4):
            line = jnp.where(
                ((row & 3) == k) & ((lane >> 5) == k), turn(rows, 32 * k - 32 * x), line
            )
        level_out[x, :, 0:128] = jnp.sum(line[0:4], axis=0, keepdims=True)
        level_out[x, :, 128:256] = jnp.sum(line[4:8], axis=0, keepdims=True)


def deliver(*refs):
    sources, results, stops, sem = refs[:3], refs[3:6], refs[6:9], refs[9]
    copies = [
        [pltpu.make_async_copy(src, dst, sem.at[leg, k]) for k, (src, dst) in enumerate(pairs)]
        for leg, pairs in enumerate((zip(sources, stops), zip(stops, results)))
    ]
    for copy in copies[0]:
        copy.start()
    for copy, onward in zip(*copies):
        copy.wait()
        onward.start()
    for copy in copies[1]:
        copy.wait()


def face_rows(pieces):
    return 8 * (pieces + 2 + 2 * ((pieces + 3) // 4))


def shards(
    particle_local_offsets,
    particle_velocity,
    stochastic_kicks,
    thermal_mesh_entry,
    occupant_tally,
    fermion_thermal_level,
    fluence_profile,
):
    vmem = pl.BlockSpec(memory_space=pltpu.VMEM)
    args = (
        particle_local_offsets.reshape(384, 16),
        particle_velocity.reshape(384, 16),
        stochastic_kicks.reshape(768, 16),
        thermal_mesh_entry.reshape(128, 16),
        occupant_tally,
        fermion_thermal_level,
        fluence_profile.T,
    )
    buffers = [
        (56, 128), (160, 128), (8, 2, 128),
        (56, 128), (160, 128), (8, 2, 128), (48, 128), (48, 128), (48, 128),
        (27, 48, 128), (9, 48, 128), (19, 48, 128), (27, 16, 128), (27, 48, 128), (16, 128), (48, 128),
        (16, 27, 16, 128), (STEPS, face_rows(6), 128), (STEPS, POS_TOTAL, 128),
        (STEPS, face_rows(2), 128), (STEPS, SLOPE_TOTAL, 128), (16, 128), (16, 128), (512, 128),
        (ROUNDS, 8, 128), (ROUNDS, len(WIDE), 8, 128), (8, 128), (len(FLAT), 8, 128),
        (FOLD, 24, 128), (FOLD, 24, 128),
        (96, 128), (96, 128), (8, 1, 128), (8, 1, 128),
    ]
    sems = [(7,), (2, 2), (2,), (STEPS, 2), (STEPS, 2), (ROUNDS, 2), (2,), (2,), (2,), (2,)]
    position, velocity, level = pl.pallas_call(
        kernel,
        out_shape=(
            jax.ShapeDtypeStruct((384, 16), F32),
            jax.ShapeDtypeStruct((384, 16), F32),
            jax.ShapeDtypeStruct(fermion_thermal_level.shape, F32),
        ),
        in_specs=[pl.BlockSpec(memory_space=pltpu.HBM)] * 7,
        out_specs=(pl.BlockSpec(memory_space=pltpu.HBM),) * 2 + (vmem,),
        scratch_shapes=[pltpu.VMEM((arg.shape[0] + 8, 16), arg.dtype) for arg in args[:4]]
        + [pltpu.VMEM(arg.shape, arg.dtype) for arg in args[4:]]
        + [pltpu.VMEM((392, 16), F32)] * 2
        + [pltpu.VMEM(shape, F32) for shape in buffers]
        + [pltpu.SemaphoreType.DMA(shape) for shape in sems],
        compiler_params=pltpu.CompilerParams(
            collective_id=0, has_side_effects=True, vmem_limit_bytes=60 * 1024 * 1024
        ),
    )(*args)
    results = (position, velocity, level)
    position, velocity, level = pl.pallas_call(
        deliver,
        out_shape=tuple(jax.ShapeDtypeStruct(result.shape, F32) for result in results),
        in_specs=[pl.BlockSpec(memory_space=pltpu.HBM)] * 3,
        out_specs=(pl.BlockSpec(memory_space=pltpu.HBM),) * 3,
        scratch_shapes=[pltpu.VMEM(result.shape, F32) for result in results]
        + [pltpu.SemaphoreType.DMA((2, 3))],
        compiler_params=pltpu.CompilerParams(vmem_limit_bytes=60 * 1024 * 1024),
    )(*results)
    shape = particle_local_offsets.shape
    return position.reshape(shape), velocity.reshape(shape), level


def solution(mesh):
    placed = (
        P(None, None, "gx", "gy", "gz"),
        P(None, None, "gx", "gy", "gz"),
        P(None, None, None, "gx", "gy", "gz"),
        P(None, "gx", "gy", "gz"),
        P("gx", "gy", "gz"),
        P("gx", ("gy", "gz"), None),
        P("gx", ("gy", "gz")),
    )
    return jax.shard_map(
        shards,
        mesh=mesh,
        in_specs=placed,
        out_specs=(
            P(None, None, "gx", "gy", "gz"),
            P(None, None, "gx", "gy", "gz"),
            P("gx", ("gy", "gz"), None),
        ),
        check_vma=False,
    )
```
